256 devices in a mesh: dp: 16 (over x_hi, y, core), mp: 16 (over z, x_lo).
Axes of the slice: x: 4 (x_hi: 2, x_lo: 2; x = x_hi * 2 + x_lo), y: 4, z: 8, core: 2. Of those that a mesh axis runs over, the one named last changes fastest.
Arguments:
- tokens: bfloat16 [8192, 6144], P(('dp', 'mp')), may hold values from -40 to 40
- norm_gain: float32 [6144], replicated, may hold values from 0.1 to 1.9
- q_gain: float32 [128], replicated, may hold values from 0.5 to 8
- k_gain: float32 [128], replicated, may hold values from 0.5 to 8
- w_query: bfloat16 [6144, 4096], P('dp', 'mp'), may hold values from -0.078125 to 0.078125
- w_key: bfloat16 [6144, 4096], P('dp', 'mp'), may hold values from -0.078125 to 0.078125
- w_value: bfloat16 [6144, 4096], P('dp', 'mp'), may hold values from -0.078125 to 0.078125
- grad_heads: bfloat16 [8192, 4096], P('dp', 'mp'), may hold values from -6 to 6
Outputs:
- grad_tokens: bfloat16 [8192, 6144], P(('dp', 'mp'))
- grad_query_weight: bfloat16 [6144, 4096], P('dp', 'mp')
- grad_key_weight: bfloat16 [6144, 4096], P('dp', 'mp')
- grad_value_weight: bfloat16 [6144, 4096], P('dp', 'mp')
The draws below stay inside these ranges and needn't reach their ends.
All inputs are finite; a program needn't handle non-finite values.
Results may differ from the reference program's by a relative error of at most 0.03.
The reference program's roundings to bfloat16 on the way (of `normed`, `values`, `attention_bf`, `grad_value` and `grad_scores`) count: a program that leaves them out, or rounds other values in their place, can miss the bound.
Values may be sent and summed in bfloat16 or wider, within the bound.
A program may use at most 128 MiB of HBM per device.

```python
import math
import jax
import jax.numpy as jnp
from jax import lax

D = 6144
H = 32
HD = 128
PATCH = 256
HH = 4096
TOK = 512
TOKENS = 8192
N_DP = 16
N_MP = 16


def draw_tokens(key, part):
    key_rows = jax.random.fold_in(key, 1)
    key_cols = jax.random.fold_in(key, 2)
    key_vals = jax.random.fold_in(key, 3)
    row_scale = jnp.exp(jax.random.uniform(key_rows, (TOKENS, 1), jnp.float32, math.log(0.3), math.log(3.0)))
    col_scale = jnp.exp(jax.random.uniform(key_cols, (1, D), jnp.float32, math.log(0.3), math.log(3.0)))
    entries = jnp.clip(jax.random.normal(key_vals, (TOKENS, D), jnp.float32), -4.0, 4.0)
    return (row_scale * col_scale * entries).astype(jnp.bfloat16)


def gain_table(key, salt):
    base_gain = jnp.exp(jax.random.uniform(jax.random.fold_in(key, salt), (HD,), jnp.float32, math.log(0.6), math.log(1.6)))
    return base_gain


def draw_q_gain(key, part):
    return gain_table(key, 21)


def draw_k_gain(key, part):
    return gain_table(key, 22)


def block_scale(own_key, extent, cuts, smallest, largest):
    gain = 1.0
    for position, shards_of in cuts:
        draws = jax.random.uniform(jax.random.fold_in(jax.random.fold_in(own_key, 6), position), (shards_of,), jnp.float32, smallest / len(cuts), largest / len(cuts))
        gain = gain * jnp.repeat(jnp.exp(draws), extent[position] // shards_of).reshape((-1,) + (1,) * (len(extent) - 1 - position))
    return gain


def noise(rng, extent, width, limit, pieces=(), held_as=jnp.bfloat16):
    result = jax.random.normal(rng, extent, jnp.float32) * width
    if len(pieces) > 0:
        result = block_scale(rng, extent, pieces, -0.22, 0.18) * result
    return jnp.clip(result, min=-limit, max=limit).astype(held_as)


def setup_inputs(seed: int = 0) -> dict:
    key_of = jax.random.split(jax.random.key(seed), 9)
    return {
        "tokens": draw_tokens(jax.random.fold_in(key_of[8], 71), 0),
        "norm_gain": jnp.clip(1.0 + 0.18 * jax.random.normal(key_of[1], (D,), jnp.float32), 0.1, 1.9),
        "q_gain": draw_q_gain(jax.random.fold_in(key_of[8], 71), 0),
        "k_gain": draw_k_gain(jax.random.fold_in(key_of[8], 71), 0),
        "w_query": noise(key_of[4], (D, HH), D ** -0.5, 0.078125, ((0, 16), (1, 16))),
        "w_key": noise(key_of[5], (D, HH), D ** -0.5, 0.078125, ((0, 16), (1, 16))),
        "w_value": noise(key_of[6], (D, HH), D ** -0.5, 0.078125, ((0, 16), (1, 16))),
        "grad_heads": noise(key_of[7], (TOKENS, HH), 1.0, 6.0, ((0, 16), (1, 16))),
    }


def normalize(row_data, gain_vector):
    average = lax.optimization_barrier(jnp.mean(row_data, axis=-1, keepdims=True))
    centred = row_data - average
    inv_spread = lax.rsqrt(lax.optimization_barrier(jnp.mean(centred * centred, axis=-1, keepdims=True)) + 1e-06)
    unit_data = centred * inv_spread
    return (unit_data * gain_vector, unit_data, inv_spread)

def normalize_back(grad_out, unit_data, inv_spread, gain_vector):
    scaled = grad_out * gain_vector
    inner_term = lax.optimization_barrier(jnp.mean(scaled * unit_data, axis=-1, keepdims=True))
    return (scaled - lax.optimization_barrier(jnp.mean(scaled, axis=-1, keepdims=True)) - unit_data * inner_term) * inv_spread

def attend_first(query_bf, key_bf, grad_out):
    factor = query_bf.shape[-1] ** (-0.5)
    scores = jnp.einsum('bqhd,bkhd->bhqk', query_bf.astype(jnp.float32), key_bf.astype(jnp.float32)) * factor
    attention = jax.nn.softmax(scores, axis=-1)
    attention_bf = attention.astype(jnp.bfloat16)
    grad_value = jnp.einsum('bhqk,bqhd->bkhd', attention_bf.astype(jnp.float32), grad_out.astype(jnp.float32)).astype(jnp.bfloat16)
    return (attention, grad_value)

def attend_rest(attention, query_bf, key_bf, value_bf, grad_out):
    factor = query_bf.shape[-1] ** (-0.5)
    grad_probs = jnp.einsum('bqhd,bkhd->bhqk', grad_out.astype(jnp.float32), value_bf.astype(jnp.float32))
    row_delta = lax.optimization_barrier(jnp.sum(attention * grad_probs, axis=-1, keepdims=True))
    grad_scores = (attention * (grad_probs - row_delta) * factor).astype(jnp.bfloat16)
    grad_query = jnp.einsum('bhqk,bkhd->bqhd', grad_scores.astype(jnp.float32), key_bf.astype(jnp.float32))
    grad_key = jnp.einsum('bhqk,bqhd->bkhd', grad_scores.astype(jnp.float32), query_bf.astype(jnp.float32))
    return (grad_query, grad_key)

def reference(tokens, norm_gain, q_gain, k_gain, w_query, w_key, w_value, grad_heads):
    normed, unit_rows, row_spread = normalize(tokens.astype(jnp.float32), norm_gain)
    normed = normed.astype(jnp.bfloat16)
    queries = jnp.dot(normed, w_query, preferred_element_type=jnp.float32)
    key_proj = jnp.dot(normed, w_key, preferred_element_type=jnp.float32)
    values = jnp.dot(normed, w_value, preferred_element_type=jnp.float32).astype(jnp.bfloat16)
    layout = (TOKENS // PATCH, PATCH, H, HD)
    query_normed, query_unit, query_spread = normalize(queries.reshape(layout), q_gain)
    key_normed, key_unit, key_spread = normalize(key_proj.reshape(layout), k_gain)
    query_bf = query_normed.astype(jnp.bfloat16)
    key_bf = key_normed.astype(jnp.bfloat16)
    grad_out = grad_heads.reshape(layout)
    attention, grad_value = attend_first(query_bf, key_bf, grad_out)
    grad_qn, grad_kn = attend_rest(attention, query_bf, key_bf, values.reshape(layout), grad_out)
    grad_query = normalize_back(grad_qn, query_unit, query_spread, q_gain).astype(jnp.bfloat16).reshape(TOKENS, HH)
    grad_key = normalize_back(grad_kn, key_unit, key_spread, k_gain).astype(jnp.bfloat16).reshape(TOKENS, HH)
    grad_value = grad_value.reshape(TOKENS, HH)
    block_cols = HH // N_MP
    grad_parts = (grad_query, grad_key, grad_value)
    weight_parts = (w_query, w_key, w_value)

    def add_block(total, block_index):
        begin_col = (block_index * block_cols).astype(jnp.int32)
        partial_sum = jnp.zeros((TOKENS, D), jnp.float32)
        for grad_item, weight_item in zip(grad_parts, weight_parts):
            grad_cols = lax.dynamic_slice_in_dim(grad_item, begin_col, block_cols, 1)
            weight_cols = lax.dynamic_slice_in_dim(weight_item, begin_col, block_cols, 1)
            partial_sum = partial_sum + jnp.dot(grad_cols, weight_cols.T, preferred_element_type=jnp.float32)
        rounded = lax.optimization_barrier(partial_sum.astype(jnp.bfloat16)).astype(jnp.float32)
        return (total + rounded, None)
    grad_normed, _ = lax.scan(add_block, jnp.zeros((TOKENS, D), jnp.float32), jnp.arange(N_MP, dtype=jnp.int32))
    grad_tokens = normalize_back(grad_normed, unit_rows, row_spread, norm_gain).astype(jnp.bfloat16)
    grouped = (normed.reshape(N_DP, TOK, D), grad_query.reshape(N_DP, TOK, HH), grad_key.reshape(N_DP, TOK, HH), grad_value.reshape(N_DP, TOK, HH))

    def accumulate(carried, group_data):
        row_block = group_data[0]
        updated = tuple((running + lax.optimization_barrier(jnp.dot(row_block.T, grad_item, preferred_element_type=jnp.float32).astype(jnp.bfloat16)).astype(jnp.float32) for running, grad_item in zip(carried, group_data[1:])))
        return (updated, None)
    zero_block = jnp.zeros((D, HH), jnp.float32)
    totals, _ = lax.scan(accumulate, (zero_block, zero_block, zero_block), grouped)
    return (grad_tokens, totals[0].astype(jnp.bfloat16), totals[1].astype(jnp.bfloat16), totals[2].astype(jnp.bfloat16))
```

```python
import jax
import jax.numpy as jnp
from jax import lax
from jax.experimental import pallas as pl
from jax.experimental.pallas import tpu as pltpu
from jax.sharding import PartitionSpec as P

MESH = pl.DeviceIdType.MESH
F32 = jnp.float32
BF16 = jnp.bfloat16
NZ, NY = 8, 4
EPS = 1e-06

NAMES = (
    ["x0", "x1"]
    + [f"{n}{k}" for n in ("af", "hf", "xf") for k in (1, 2, 3, 4)]
    + [f"{n}{k}" for n in ("ab", "hb", "xb") for k in (1, 2, 3)]
    + ["wx"]
    + [f"{n}{k}" for n in ("wf1", "wf2", "wb1", "ws0", "wsf1", "wsf2", "wsb1") for k in (0, 1)]
    + [f"px{k}" for k in range(9)]
    + [f"{n}{k}" for n in ("paf", "phf") for k in (1, 2, 3, 4)]
    + [f"{n}{k}" for n in ("pab", "phb") for k in (1, 2, 3)]
    + [f"gs{k}" for k in range(8)]
    + [f"gy{k}" for k in range(6)]
    + ["gx"]
)
ID = {name: i for i, name in enumerate(NAMES)}


def dot(a, b, contract):
    return lax.dot_general(a, b, (contract, ((), ())), preferred_element_type=F32)


def unit(rows):
    centred = rows - jnp.mean(rows, axis=-1, keepdims=True)
    inv = lax.rsqrt(jnp.mean(centred * centred, axis=-1, keepdims=True) + EPS)
    return centred * inv, inv


def unit_back(grad, rows_unit, inv, gain):
    e = grad * gain
    inner = jnp.mean(e * rows_unit, axis=-1, keepdims=True)
    return (e - jnp.mean(e, axis=-1, keepdims=True) - rows_unit * inner) * inv


def kernel(
    tok, gain, qg, kg, wq, wk, wv, gh,
    out_tok, out_q, out_k, out_v,
    nrm, wts, part, gwt, rz, rx, rs, ry, rh, acc, grd, grt, go, send, recv, local,
):
    d, m = lax.axis_index("dp"), lax.axis_index("mp")
    core, y, xh = lax.rem(d, 2), lax.rem(d // 2, NY), d // (2 * NY)
    z, xl = m // 2, lax.rem(m, 2)
    s = 1 - 2 * core

    def zo(o):
        return lax.rem(z + o * s + NZ, NZ)

    def yo(o):
        return lax.rem(y + o * s + NY, NY)

    def dp(x_other, yy, c=core):
        return ((lax.rem(xh + x_other, 2)) * NY + yy) * 2 + c

    to_zf, to_zb, to_x = (d, zo(1) * 2 + xl), (d, zo(-1) * 2 + xl), (d, z * 2 + 1 - xl)
    to_yf, to_yb = (dp(0, yo(1)), m), (dp(0, yo(-1)), m)
    to_s, to_h = (dp(0, y, 1 - core), m), (dp(1, y), m)
    started = []

    def put(name, src, dst, device, land=None):
        copy = pltpu.make_async_remote_copy(
            src_ref=src, dst_ref=dst, send_sem=send.at[ID[name]], recv_sem=recv.at[ID[land or name]],
            device_id=device, device_id_type=MESH,
        )
        copy.start()
        started.append(copy)

    def got(name, dst):
        pltpu.make_async_remote_copy(
            src_ref=dst, dst_ref=dst, send_sem=send.at[ID[name]], recv_sem=recv.at[ID[name]],
            device_id=to_s, device_id_type=MESH,
        ).wait_recv()

    own = [
        pltpu.make_async_copy(w, wts.at[d, :, pl.ds(256 * i, 256)], local.at[i])
        for i, w in enumerate((wq, wk, wv))
    ]
    for copy in own:
        copy.start()
    heads_in = pltpu.make_async_copy(gh, go, local.at[3])
    heads_in.start()

    barrier = pltpu.get_barrier_semaphore()
    for device in (to_zf, to_zb, to_x, to_yf, to_yb, to_s, to_h):
        pl.semaphore_signal(barrier, inc=1, device_id=device, device_id_type=MESH)

    rows, _ = unit(tok[...].astype(F32))
    normed = (rows * gain[...]).astype(BF16)
    nrm[z, 0, xl] = normed[:16]
    nrm[z, 1, xl] = normed[16:]
    pl.semaphore_wait(barrier, 7)

    put("x0", nrm.at[z, 0, xl], nrm.at[z, 0, xl], to_x)
    put("af1", nrm.at[z, 1, xl], nrm.at[z, 1, xl], to_zf)
    put("ab1", nrm.at[z, 1, xl], nrm.at[z, 1, xl], to_zb)
    for copy in own:
        copy.wait()

    def put_w(name, block, device):
        put(name, wts.at[block], wts.at[block], device)

    put_w("wx", d, to_h)
    put_w("wf10", d, to_yf)
    put_w("wb10", d, to_yb)
    put_w("ws00", d, to_s)
    put("x1", nrm.at[z, 1, xl], nrm.at[z, 1, xl], to_x)

    def tokens_a(k, back):
        zz = zo(k) if back else zo(-k)
        block = nrm.at[zz, 1, xl]
        got(f"a{'b' if back else 'f'}{k}", block)
        if back and k < 3:
            put(f"ab{k + 1}", block, block, to_zb)
        if not back and k < 4:
            put(f"af{k + 1}", block, block, to_zf)
        put(f"x{'b' if back else 'f'}{k}", block, block, to_x)

    def tokens_h(k, back):
        zz = zo(k) if back else zo(-k)
        block = nrm.at[zz, 0]
        got(f"h{'b' if back else 'f'}{k}", block)
        if back and k < 3:
            put(f"hb{k + 1}", block, block, to_zb)
        if not back and k < 4:
            put(f"hf{k + 1}", block, block, to_zf)

    def weights(kind, x):
        block = dp(x, yo({"f1": -1, "f2": -2, "b1": 1}[kind]))
        got(f"w{kind}{x}", wts.at[block])
        if kind == "f1":
            put_w(f"wf2{x}", block, to_yf)
        put_w(f"ws{kind}{x}", block, to_s)

    got("x0", nrm.at[z, 0, 1 - xl])
    put("hf1", nrm.at[z, 0], nrm.at[z, 0], to_zf)
    put("hb1", nrm.at[z, 0], nrm.at[z, 0], to_zb)
    tokens_a(1, False)
    tokens_a(1, True)
    other = dp(1, y)
    got("wx", wts.at[other])
    put_w("wf11", other, to_yf)
    put_w("wb11", other, to_yb)
    put_w("ws01", other, to_s)
    weights("f1", 0)
    weights("b1", 0)
    tokens_h(1, False)
    tokens_h(1, True)
    tokens_a(2, False)
    tokens_a(2, True)
    weights("f1", 1)
    weights("b1", 1)
    tokens_h(2, False)
    tokens_h(2, True)
    tokens_a(3, False)
    tokens_a(3, True)
    weights("f2", 0)
    tokens_h(3, False)
    tokens_h(3, True)
    tokens_a(4, False)
    weights("f2", 1)
    tokens_h(4, False)
    got("x1", nrm.at[z, 1, 1 - xl])
    for k in (1, 2, 3, 4):
        got(f"xf{k}", nrm.at[zo(-k), 1, 1 - xl])
    for k in (1, 2, 3):
        got(f"xb{k}", nrm.at[zo(k), 1, 1 - xl])
    for x in (0, 1):
        got(f"ws0{x}", wts.at[dp(x, y, 1 - core)])
        got(f"wsf1{x}", wts.at[dp(x, yo(1), 1 - core)])
        got(f"wsb1{x}", wts.at[dp(x, yo(-1), 1 - core)])
        got(f"wsf2{x}", wts.at[dp(x, yo(2), 1 - core)])

    def columns(j):
        start = pl.multiple_of(j * 768, 768)
        return nrm[:, :, :, :, pl.ds(start, 768)].reshape(512, 768)

    acc[...] = dot(columns(0), wts[0:2].reshape(768, 768), ((1,), (0,)))

    @pl.loop(1, 8)
    def _(j):
        acc[...] += dot(columns(j), wts[pl.ds(2 * j, 2)].reshape(768, 768), ((1,), (0,)))

    heads_in.wait()
    q_gain, k_gain = qg[...], kg[...]

    @pl.loop(0, 2)
    def _(image):
        r = pl.ds(pl.multiple_of(image * 256, 256), 256)
        for h in (0, 1):
            q_unit, q_inv = unit(acc[r, h * 128 : h * 128 + 128])
            k_unit, k_inv = unit(acc[r, 256 + h * 128 : 384 + h * 128])
            value = acc[r, 512 + h * 128 : 640 + h * 128].astype(BF16)
            qn, kn = (q_unit * q_gain).astype(BF16), (k_unit * k_gain).astype(BF16)
            cot = go[r, h * 128 : h * 128 + 128]
            cot = jnp.concatenate(
                [cot[64 * a + 32 * c + 16 * b :][:16] for a in range(4) for b in range(2) for c in range(2)],
                axis=0,
            )
            scores = dot(qn, kn, ((1,), (1,))) * (128**-0.5)
            e = jnp.exp(scores - jnp.max(scores, axis=-1, keepdims=True))
            att = e / jnp.sum(e, axis=-1, keepdims=True)
            grad_v = dot(att.astype(BF16), cot, ((0,), (0,)))
            grad_p = dot(cot, value, ((1,), (1,)))
            delta = jnp.sum(att * grad_p, axis=-1, keepdims=True)
            grad_s = (att * (grad_p - delta) * (128**-0.5)).astype(BF16)
            grad_q = unit_back(dot(grad_s, kn, ((1,), (0,))), q_unit, q_inv, q_gain)
            grad_k = unit_back(dot(grad_s, qn, ((0,), (0,))), k_unit, k_inv, k_gain)
            for i, g in enumerate((grad_q, grad_k, grad_v)):
                c0 = i * 256 + h * 128
                grd[pl.ds(image * 4, 4), :, c0 : c0 + 128] = g.astype(BF16).reshape(4, 64, 128)
                grt[c0 : c0 + 128, r] = g.T.astype(BF16)

    def make_part(o1, o2):
        left = jnp.concatenate([grd[zo(o1)], grd[zo(o2)]], axis=0)

        @pl.loop(0, 8)
        def _(j):
            cols = pl.ds(pl.multiple_of(j * 768, 768), 768)
            p = dot(left, wts[pl.ds(2 * j, 2)].reshape(768, 768), ((1,), (1,))).astype(BF16)
            part[zo(o1), :, :, :, cols] = p[:64].reshape(2, 2, 16, 768)
            part[zo(o2), :, :, :, cols] = p[64:].reshape(2, 2, 16, 768)

        for o in (o1, o2):
            put(f"px{o % 8}", part.at[zo(o), 1, 1 - xl], rx.at[o % 8], to_x)

    def make_gw(o, x):
        j = lax.rem(xh + x, 2) * NY + yo(o)
        right = columns(j)

        @pl.loop(0, 3)
        def _(i):
            r = pl.ds(pl.multiple_of(i * 256, 256), 256)
            p = dot(grt[r, :], right, ((1,), (0,))).astype(BF16)
            gwt[2 * j, r, :] = p[:, :384]
            gwt[2 * j + 1, r, :] = p[:, 384:]

        there = (-o % 4) * 2 + x
        put(f"gs{(o % 4) * 2 + x}", gwt.at[2 * j + 1 - core], rs.at[there], to_s, f"gs{there}")

    def add(dst, *terms):
        total = dst[...].astype(F32)
        for t in terms:
            total = total + t[...].astype(F32)
        dst[...] = total.astype(BF16)

    def add_gw(o, x, y_names):
        block = gwt.at[dp(x, yo(o))]
        slot = (o % 4) * 2 + x
        got(f"gs{slot}", rs.at[slot])
        for n in y_names:
            got(f"gy{n}", ry.at[n])

        @pl.loop(0, 3)
        def _(i):
            r = pl.ds(pl.multiple_of(i * 256, 256), 256)
            add(block.at[r], rs.at[slot, r], *[ry.at[n, r] for n in y_names])

        return block

    def chain_a(o, slot):
        block = part.at[zo(o), 1, xl]
        got(f"px{o % 8}", rx.at[o % 8])
        terms = [rx.at[o % 8]]
        if slot is not None:
            got(("paf%d" % (slot + 1)) if slot < 4 else ("pab%d" % (slot - 3)), rz.at[slot, 2])
            terms.append(rz.at[slot, 2])
        add(block, *terms)
        if o > 0:
            put(f"paf{5 - o}", block, rz.at[4 - o, 2], to_zf)
        else:
            put(f"pab{4 + o}", block, rz.at[7 + o, 2], to_zb)

    def chain_h(o, slot):
        block = part.at[zo(o), 0]
        if slot is not None:
            got(("phf%d" % (slot + 1)) if slot < 4 else ("phb%d" % (slot - 3)), rz.at[slot, pl.ds(0, 2)])
            add(block, rz.at[slot, pl.ds(0, 2)])
        if o > 0:
            put(f"phf{5 - o}", block, rz.at[4 - o, pl.ds(0, 2)], to_zf)
        else:
            put(f"phb{4 + o}", block, rz.at[7 + o, pl.ds(0, 2)], to_zb)

    make_part(4, 3)
    chain_h(4, None)
    make_gw(2, 1)
    make_gw(2, 0)
    chain_a(4, None)
    make_part(-3, 2)
    chain_h(-3, None)
    make_gw(1, 1)
    make_gw(-1, 1)
    put("gy1", add_gw(2, 1, ()), ry.at[1], to_yf)
    put("gy0", add_gw(2, 0, ()), ry.at[0], to_yf)
    chain_a(-3, None)
    make_gw(1, 0)
    make_gw(-1, 0)
    put("gy5", add_gw(-1, 1, ()), ry.at[5], to_yb)
    chain_h(3, 0)
    chain_a(3, 0)
    make_part(-2, 1)
    put("gy4", add_gw(-1, 0, ()), ry.at[4], to_yb)
    chain_h(-2, 4)
    chain_a(-2, 4)
    make_gw(0, 1)
    make_gw(0, 0)
    put("gy3", add_gw(1, 1, (1,)), ry.at[3], to_yf)
    make_part(-1, 0)
    put("gy2", add_gw(1, 0, (0,)), ry.at[2], to_yf)
    chain_h(2, 1)
    chain_a(2, 1)
    chain_h(-1, 5)
    chain_a(-1, 5)
    put("gx", add_gw(0, 1, (3, 5)), rh, to_h)
    chain_h(1, 2)
    chain_a(1, 2)

    got("phb3", rz.at[6, pl.ds(0, 2)])
    got("phf4", rz.at[3, pl.ds(0, 2)])
    add(part.at[z, 0, 1 - xl], rz.at[6, 1 - xl], rz.at[3, 1 - xl])
    put("px8", part.at[z, 0, 1 - xl], rx.at[8], to_x)

    slot = 0
    got("gs0", rs.at[0])
    got("gy2", ry.at[2])
    got("gy4", ry.at[4])
    got("gx", rh)
    for i, out in enumerate((out_q, out_k, out_v)):
        r = pl.ds(256 * i, 256)
        total = gwt[d, r].astype(F32) + rs[slot, r].astype(F32)
        total += ry[2, r].astype(F32) + ry[4, r].astype(F32) + rh[r].astype(F32)
        out[...] = total.T.astype(BF16)

    got("px0", rx.at[0])
    got("pab3", rz.at[6, 2])
    got("paf4", rz.at[3, 2])
    got("px8", rx.at[8])
    half0 = part[z, 0, xl].astype(F32) + rz[6, xl].astype(F32) + rz[3, xl].astype(F32) + rx[8].astype(F32)
    half1 = part[z, 1, xl].astype(F32) + rz[6, 2].astype(F32) + rz[3, 2].astype(F32) + rx[0].astype(F32)
    for i, grad in enumerate((half0, half1)):
        rows, inv = unit(tok[16 * i : 16 * i + 16, :].astype(F32))
        out_tok[16 * i : 16 * i + 16, :] = unit_back(grad, rows, inv, gain[...]).astype(BF16)

    for copy in started:
        copy.wait_send()


def per_device(tokens, norm_gain, q_gain, k_gain, w_query, w_key, w_value, grad_heads):
    vmem, anywhere = pl.BlockSpec(memory_space=pltpu.VMEM), pl.BlockSpec(memory_space=pl.ANY)
    count = len(NAMES)
    return pl.pallas_call(
        kernel,
        out_shape=[
            jax.ShapeDtypeStruct(tokens.shape, BF16),
            jax.ShapeDtypeStruct(w_query.shape, BF16),
            jax.ShapeDtypeStruct(w_key.shape, BF16),
            jax.ShapeDtypeStruct(w_value.shape, BF16),
        ],
        in_specs=[vmem] * 4 + [anywhere] * 4,
        out_specs=[vmem] * 4,
        scratch_shapes=[
            pltpu.VMEM((8, 2, 2, 16, 6144), BF16),
            pltpu.VMEM((16, 384, 768), BF16),
            pltpu.VMEM((8, 2, 2, 16, 6144), BF16),
            pltpu.VMEM((16, 768, 384), BF16),
            pltpu.VMEM((7, 3, 16, 6144), BF16),
            pltpu.VMEM((9, 16, 6144), BF16),
            pltpu.VMEM((8, 768, 384), BF16),
            pltpu.VMEM((6, 768, 384), BF16),
            pltpu.VMEM((768, 384), BF16),
            pltpu.VMEM((512, 768), F32),
            pltpu.VMEM((8, 64, 768), BF16),
            pltpu.VMEM((768, 512), BF16),
            pltpu.VMEM((512, 256), BF16),
            pltpu.SemaphoreType.DMA((count,)),
            pltpu.SemaphoreType.DMA((count,)),
            pltpu.SemaphoreType.DMA((4,)),
        ],
        compiler_params=pltpu.CompilerParams(
            collective_id=0, has_side_effects=True, vmem_limit_bytes=64 * 1024 * 1024 - 65536
        ),
        cost_estimate=pl.CostEstimate(flops=15_000_000_000, bytes_accessed=3_000_000, transcendentals=300_000),
        name="attention_branch_back",
    )(
        tokens, norm_gain.reshape(1, -1), q_gain.reshape(1, -1), k_gain.reshape(1, -1),
        w_query, w_key, w_value, grad_heads,
    )


def solution(mesh):
    placed = (
        P(("dp", "mp"), None),
        P(),
        P(),
        P(),
        P("dp", "mp"),
        P("dp", "mp"),
        P("dp", "mp"),
        P("dp", "mp"),
    )
    return jax.shard_map(
        per_device,
        mesh=mesh,
        in_specs=placed,
        out_specs=(P(("dp", "mp"), None), P("dp", "mp"), P("dp", "mp"), P("dp", "mp")),
        check_vma=False,
    )
```

```python
import jax
import jax.numpy as jnp
from jax import lax
from jax.experimental import pallas as pl
from jax.experimental.pallas import tpu as pltpu
from jax.sharding import PartitionSpec as P

MESH = pl.DeviceIdType.MESH
F32 = jnp.float32
BF16 = jnp.bfloat16
NZ, NY = 8, 4
EPS = 1e-06

SPAN = {"A0": (0, 1536), "A1": (1536, 2688), "H0": (2688, 4992), "H1": (4992, 6144)}
A_COLS, H_COLS = 2688, 3456
STEPS = [("f", k) for k in (1, 2, 3, 4)] + [("b", k) for k in (1, 2, 3)]

NAMES = (
    [f"xo{g}" for g in SPAN]
    + [f"{t}{g}{w}{k}" for t in ("t", "p") for g in SPAN for w, k in STEPS]
    + [f"x{g}{w}{k}" for g in ("A0", "A1") for w, k in STEPS]
    + ["wx"]
    + [f"{n}{k}" for n in ("wf1", "wf2", "wb1", "ws0", "wsf1", "wsf2", "wsb1") for k in (0, 1)]
    + [f"px{g}{k}" for g in ("A0", "A1") for k in range(8)]
    + ["fxH0", "fxH1"]
    + [f"gs{k}" for k in range(8)]
    + [f"gy{k}" for k in range(6)]
    + ["gx"]
)
ID = {name: i for i, name in enumerate(NAMES)}

GATHER = (
    "A0f1", "A0b1", "A1f1", "oH0", "A1b1", "oH1", "A0f2", "A0b2",
    "A1f2", "wf10", "H0f1", "H0b1", "wb10", "A1b2", "H1f1", "H1b1",
    "wx", "A0f3", "A0b3", "wf20", "A1f3", "H0f2", "wf11", "H0b2",
    "A1b3", "H1f2", "H1b2", "A0f4", "A1f4", "wb11", "H0f3", "H0b3",
    "wf21", "H1f3", "H1b3", "H0f4", "H1f4",
)
SUM = (
    "PH1", "PA1", "G21", "H1f1", "G31", "G11", "A1f0", "H1b1",
    "PH0", "D21", "A1b0", "A1f1", "H1f2", "H1b2", "PA0", "G01",
    "D31", "H0f1", "G20", "G00", "H0b1", "G30", "D11", "A0f0",
    "A1f2", "A1b1", "G10", "A0b0", "H1f3", "H0f2", "D20", "H0b2",
    "A0f1", "A1f3", "D01", "A0b1", "A1b2", "H1pre", "D30", "H0f3",
    "D10", "A0f2", "A0b2", "A1fin", "H0pre", "A0f3", "H1fin", "D00",
    "A0fin", "H0fin",
)


def dot(a, b, contract):
    return lax.dot_general(a, b, (contract, ((), ())), preferred_element_type=F32)


def unit(rows):
    centred = rows - jnp.mean(rows, axis=-1, keepdims=True)
    inv = lax.rsqrt(jnp.mean(centred * centred, axis=-1, keepdims=True) + EPS)
    return centred * inv, inv


def unit_back(grad, rows_unit, inv, gain):
    e = grad * gain
    inner = jnp.mean(e * rows_unit, axis=-1, keepdims=True)
    return (e - jnp.mean(e, axis=-1, keepdims=True) - rows_unit * inner) * inv


def kernel(
    tok_in, gain, qg, kg, wq, wk, wv, gh,
    out_tok, out_q, out_k, out_v,
    tok, nrm, wts, part, gwt, rzh, rza, rxa, rxh, rs, ry, rh, acc, grd, grt, go, gsum, send, recv, local,
):
    d, m = lax.axis_index("dp"), lax.axis_index("mp")
    core, y, xh = lax.rem(d, 2), lax.rem(d // 2, NY), d // (2 * NY)
    z, xl = m // 2, lax.rem(m, 2)
    s = 1 - 2 * core

    def zo(o):
        return lax.rem(z + o * s + NZ, NZ)

    def yo(o):
        return lax.rem(y + o * s + NY, NY)

    def dp(x_other, yy, c=core):
        return ((lax.rem(xh + x_other, 2)) * NY + yy) * 2 + c

    to_zf, to_zb, to_x = (d, zo(1) * 2 + xl), (d, zo(-1) * 2 + xl), (d, z * 2 + 1 - xl)
    to_yf, to_yb = (dp(0, yo(1)), m), (dp(0, yo(-1)), m)
    to_s, to_h = (dp(0, y, 1 - core), m), (dp(1, y), m)
    started = []

    def put(name, src, dst, device, land=None):
        copy = pltpu.make_async_remote_copy(
            src_ref=src, dst_ref=dst, send_sem=send.at[ID[name]], recv_sem=recv.at[ID[land or name]],
            device_id=device, device_id_type=MESH,
        )
        copy.start()
        started.append(copy)

    def got(name, dst):
        pltpu.make_async_remote_copy(
            src_ref=dst, dst_ref=dst, send_sem=send.at[ID[name]], recv_sem=recv.at[ID[name]],
            device_id=to_s, device_id_type=MESH,
        ).wait_recv()

    tok_copy = pltpu.make_async_copy(tok_in, tok, local.at[4])
    tok_copy.start()
    own = [
        pltpu.make_async_copy(w, wts.at[d, :, pl.ds(256 * i, 256)], local.at[i])
        for i, w in enumerate((wq, wk, wv))
    ]
    for copy in own:
        copy.start()
    heads_in = pltpu.make_async_copy(gh, go, local.at[3])
    heads_in.start()

    barrier = pltpu.get_barrier_semaphore()
    for device in (to_zf, to_zb, to_x, to_yf, to_yb, to_s, to_h):
        pl.semaphore_signal(barrier, inc=1, device_id=device, device_id_type=MESH)

    tok_copy.wait()
    rows, _ = unit(tok[...].astype(F32))
    nrm[z, xl] = (rows * gain[...]).astype(BF16)
    pl.semaphore_wait(barrier, 7)

    def span(g):
        return pl.ds(SPAN[g][0], SPAN[g][1] - SPAN[g][0])

    def tokens_at(g, zz):
        return nrm.at[zz, xl, :, span(g)] if g[0] == "A" else nrm.at[zz, :, :, span(g)]

    def put_same(name, block, device):
        put(name, block, block, device)

    def put_w(name, block, device):
        put(name, wts.at[block], wts.at[block], device)

    def put_x(g):
        put_same(f"xo{g}", nrm.at[z, xl, :, span(g)], to_x)

    def put_z(g):
        put_same(f"t{g}f1", tokens_at(g, z), to_zf)
        put_same(f"t{g}b1", tokens_at(g, z), to_zb)

    def tokens_step(g, way, k):
        block = tokens_at(g, zo(-k if way == "f" else k))
        got(f"t{g}{way}{k}", block)
        if k < (4 if way == "f" else 3):
            put_same(f"t{g}{way}{k + 1}", block, to_zf if way == "f" else to_zb)
        if g[0] == "A":
            put_same(f"x{g}{way}{k}", block, to_x)

    def weights_step(kind, x):
        block = dp(x, yo({"f1": -1, "f2": -2, "b1": 1}[kind]))
        got(f"w{kind}{x}", wts.at[block])
        if kind == "f1":
            put_w(f"wf2{x}", block, to_yf)
        put_w(f"ws{kind}{x}", block, to_s)

    put_x("H0")
    put_z("A0")
    put_z("A1")
    for copy in own:
        copy.wait()
    put_w("wf10", d, to_yf)
    put_w("wb10", d, to_yb)
    put_x("H1")
    put_w("wx", d, to_h)
    put_w("ws00", d, to_s)
    put_x("A0")
    put_x("A1")
    for event in GATHER:
        if event[0] == "o":
            got(f"x{event}", nrm.at[z, 1 - xl, :, span(event[1:])])
            put_z(event[1:])
        elif event == "wx":
            block = dp(1, y)
            got("wx", wts.at[block])
            put_w("wf11", block, to_yf)
            put_w("wb11", block, to_yb)
            put_w("ws01", block, to_s)
        elif event[0] == "w":
            weights_step(event[1:3], int(event[3]))
        else:
            tokens_step(event[:2], event[2], int(event[3]))
    for g in ("A0", "A1"):
        got(f"xo{g}", nrm.at[z, 1 - xl, :, span(g)])
        for way, k in STEPS:
            got(f"x{g}{way}{k}", nrm.at[zo(-k if way == "f" else k), 1 - xl, :, span(g)])
    for x in (0, 1):
        got(f"ws0{x}", wts.at[dp(x, y, 1 - core)])
        got(f"wsf1{x}", wts.at[dp(x, yo(1), 1 - core)])
        got(f"wsb1{x}", wts.at[dp(x, yo(-1), 1 - core)])
        got(f"wsf2{x}", wts.at[dp(x, yo(2), 1 - core)])

    def columns(j):
        start = pl.multiple_of(j * 768, 768)
        return nrm[:, :, :, pl.ds(start, 768)].reshape(512, 768)

    acc[...] = dot(columns(0), wts[0:2].reshape(768, 768), ((1,), (0,)))

    @pl.loop(1, 8)
    def _(j):
        acc[...] += dot(columns(j), wts[pl.ds(2 * j, 2)].reshape(768, 768), ((1,), (0,)))

    heads_in.wait()
    q_gain, k_gain = qg[...], kg[...]

    for image in (0, 1):
        r = slice(image * 256, image * 256 + 256)
        for h in (0, 1):
            q_unit, q_inv = unit(acc[r, h * 128 : h * 128 + 128])
            k_unit, k_inv = unit(acc[r, 256 + h * 128 : 384 + h * 128])
            value = acc[r, 512 + h * 128 : 640 + h * 128].astype(BF16)
            qn, kn = (q_unit * q_gain).astype(BF16), (k_unit * k_gain).astype(BF16)
            cot = go[r, h * 128 : h * 128 + 128]
            scores = dot(qn, kn, ((1,), (1,))) * (128**-0.5)
            e = jnp.exp(scores - jnp.max(scores, axis=-1, keepdims=True))
            att = e / jnp.sum(e, axis=-1, keepdims=True)
            grad_v = dot(att.astype(BF16), cot, ((0,), (0,)))
            grad_p = dot(cot, value, ((1,), (1,)))
            delta = jnp.sum(att * grad_p, axis=-1, keepdims=True)
            grad_s = (att * (grad_p - delta) * (128**-0.5)).astype(BF16)
            grad_q = unit_back(dot(grad_s, kn, ((1,), (0,))), q_unit, q_inv, q_gain)
            grad_k = unit_back(dot(grad_s, qn, ((0,), (0,))), k_unit, k_inv, k_gain)
            for i, g in enumerate((grad_q, grad_k, grad_v)):
                c0 = i * 256 + h * 128
                grd[r, c0 : c0 + 128] = g.astype(BF16)
                grt[c0 : c0 + 128, r] = g.T.astype(BF16)

    offsets = (4, -3, 3, -2, 2, -1, 1, 0)

    def make_part(g):
        first, last = SPAN[g][0] // 384, SPAN[g][1] // 384
        blocks = 2 if (last - first) % 2 == 0 else last - first
        width = blocks * 384

        @pl.loop(0, (last - first) // blocks)
        def _(i):
            w = wts[pl.ds(first + i * blocks, blocks)].reshape(width, 768)
            cols = pl.ds(pl.multiple_of(SPAN[g][0] + i * width, 128), width)
            part[:, :, :, cols] = dot(grd[...], w, ((1,), (1,))).astype(BF16).reshape(8, 2, 32, width)

        if g[0] == "A":
            for o in offsets:
                put(f"px{g}{o % 8}", part.at[zo(o), 1 - xl, :, span(g)], rxa.at[o % 8, :, span(g)], to_x)
        else:
            chain(g, "f", 0)
            chain(g, "b", 0)

    def make_gw(o, x):
        j = lax.rem(xh + x, 2) * NY + yo(o)
        p = dot(grt[...], columns(j), ((1,), (0,))).astype(BF16)
        gwt[2 * j] = p[:, :384]
        gwt[2 * j + 1] = p[:, 384:]
        there = (-o % 4) * 2 + x
        put(f"gs{(o % 4) * 2 + x}", gwt.at[2 * j + 1 - core], rs.at[there], to_s, f"gs{there}")

    def add(dst, *terms):
        total = dst[...].astype(F32)
        for t in terms:
            total = total + t[...].astype(F32)
        dst[...] = total.astype(BF16)

    def landing(g, way, k):
        slot = k - 1 if way == "f" else 3 + k
        start, end = SPAN[g]
        if g[0] == "A":
            return rza.at[slot, :, pl.ds(start, end - start)]
        return rzh.at[slot, :, :, pl.ds(start - A_COLS, end - start)]

    def chain(g, way, k):
        o = 4 - k if way == "f" else k - 3
        block = part.at[zo(o), xl, :, span(g)] if g[0] == "A" else part.at[zo(o), :, :, span(g)]
        terms = []
        if g[0] == "A":
            got(f"px{g}{o % 8}", rxa.at[o % 8, :, span(g)])
            terms.append(rxa.at[o % 8, :, span(g)])
        if k > 0:
            got(f"p{g}{way}{k}", landing(g, way, k))
            terms.append(landing(g, way, k))
        if terms:
            add(block, *terms)
        put(f"p{g}{way}{k + 1}", block, landing(g, way, k + 1), to_zf if way == "f" else to_zb)

    def chain_end(g):
        got(f"p{g}b3", landing(g, "b", 3))
        got(f"p{g}f4", landing(g, "f", 4))
        if g[0] == "H":
            block = part.at[z, 1 - xl, :, span(g)]
            add(block, landing(g, "b", 3).at[1 - xl], landing(g, "f", 4).at[1 - xl])
            put(f"fx{g}", block, rxh.at[:, pl.ds(SPAN[g][0] - A_COLS, SPAN[g][1] - SPAN[g][0])], to_x)

    def finish_tokens(g):
        back, ahead = landing(g, "b", 3), landing(g, "f", 4)
        if g[0] == "A":
            chain_end(g)
            over = rxa.at[0, :, span(g)]
            got(f"px{g}0", over)
        else:
            back, ahead = back.at[xl], ahead.at[xl]
            over = rxh.at[:, pl.ds(SPAN[g][0] - A_COLS, SPAN[g][1] - SPAN[g][0])]
            got(f"fx{g}", over)
        total = part[z, xl, :, span(g)].astype(F32) + back[...].astype(F32)
        gsum[:, span(g)] = total + ahead[...].astype(F32) + over[...].astype(F32)

    def add_gw(o, x):
        slot = (o % 4) * 2 + x
        got(f"gs{slot}", rs.at[slot])
        arrivals = {1: (x,), 0: (2 + x, 4 + x)}.get(o, ())
        for n in arrivals:
            got(f"gy{n}", ry.at[n])
        if o == 0 and x == 0:
            got("gx", rh)
            for i, out in enumerate((out_q, out_k, out_v)):
                r = pl.ds(256 * i, 256)
                total = gwt[d, r].astype(F32) + rs[0, r].astype(F32)
                total += ry[2, r].astype(F32) + ry[4, r].astype(F32) + rh[r].astype(F32)
                out[...] = total.T.astype(BF16)
            return
        block = gwt.at[dp(x, yo(o))]

        @pl.loop(0, 3)
        def _(i):
            r = pl.ds(pl.multiple_of(i * 256, 256), 256)
            add(block.at[r], rs.at[slot, r], *[ry.at[n, r] for n in arrivals])

        if o == 0:
            put("gx", block, rh, to_h)
        else:
            n = {2: 0, 1: 2, -1: 4}[o] + x
            put(f"gy{n}", block, ry.at[n], to_yb if o == -1 else to_yf)

    for event in SUM:
        if event[0] == "P":
            make_part(event[1:])
        elif event[0] in "GD":
            (make_gw if event[0] == "G" else add_gw)({"3": -1}.get(event[1], int(event[1])), int(event[2]))
        elif event[2:] == "pre":
            chain_end(event[:2])
        elif event[2:] == "fin":
            finish_tokens(event[:2])
        else:
            chain(event[:2], event[2], int(event[3]))

    rows, inv = unit(tok[...].astype(F32))
    out_tok[...] = unit_back(gsum[...], rows, inv, gain[...]).astype(BF16)

    for copy in started:
        copy.wait_send()


def hand_on(*refs):
    ins, outs, sems = refs[:4], refs[4:8], refs[8]
    copies = [pltpu.make_async_copy(a, b, sems.at[i]) for i, (a, b) in enumerate(zip(ins, outs))]
    for copy in copies:
        copy.start()
    for copy in copies:
        copy.wait()


def per_device(tokens, norm_gain, q_gain, k_gain, w_query, w_key, w_value, grad_heads):
    vmem, anywhere = pl.BlockSpec(memory_space=pltpu.VMEM), pl.BlockSpec(memory_space=pl.ANY)
    count = len(NAMES)
    shapes = [jax.ShapeDtypeStruct(a.shape, BF16) for a in (tokens, w_query, w_key, w_value)]
    results = pl.pallas_call(
        kernel,
        out_shape=shapes,
        in_specs=[anywhere] + [vmem] * 3 + [anywhere] * 4,
        out_specs=[vmem] * 4,
        scratch_shapes=[
            pltpu.VMEM((32, 6144), BF16),
            pltpu.VMEM((8, 2, 32, 6144), BF16),
            pltpu.VMEM((16, 384, 768), BF16),
            pltpu.VMEM((8, 2, 32, 6144), BF16),
            pltpu.VMEM((16, 768, 384), BF16),
            pltpu.VMEM((7, 2, 32, H_COLS), BF16),
            pltpu.VMEM((7, 32, A_COLS), BF16),
            pltpu.VMEM((8, 32, A_COLS), BF16),
            pltpu.VMEM((32, H_COLS), BF16),
            pltpu.VMEM((8, 768, 384), BF16),
            pltpu.VMEM((6, 768, 384), BF16),
            pltpu.VMEM((768, 384), BF16),
            pltpu.VMEM((512, 768), F32),
            pltpu.VMEM((512, 768), BF16),
            pltpu.VMEM((768, 512), BF16),
            pltpu.VMEM((512, 256), BF16),
            pltpu.VMEM((32, 6144), F32),
            pltpu.SemaphoreType.DMA((count,)),
            pltpu.SemaphoreType.DMA((count,)),
            pltpu.SemaphoreType.DMA((5,)),
        ],
        compiler_params=pltpu.CompilerParams(
            collective_id=0, has_side_effects=True, vmem_limit_bytes=64 * 1024 * 1024 - 65536
        ),
        cost_estimate=pl.CostEstimate(flops=15_000_000_000, bytes_accessed=3_000_000, transcendentals=300_000),
        name="attention_branch_back",
    )(
        tokens, norm_gain.reshape(1, -1), q_gain.reshape(1, -1), k_gain.reshape(1, -1),
        w_query, w_key, w_value, grad_heads,
    )
    return pl.pallas_call(
        hand_on,
        out_shape=shapes,
        in_specs=[vmem] * 4,
        out_specs=[anywhere] * 4,
        scratch_shapes=[pltpu.SemaphoreType.DMA((4,))],
        name="hand_on",
    )(*results)


def solution(mesh):
    placed = (
        P(("dp", "mp"), None),
        P(),
        P(),
        P(),
        P("dp", "mp"),
        P("dp", "mp"),
        P("dp", "mp"),
        P("dp", "mp"),
    )
    return jax.shard_map(
        per_device,
        mesh=mesh,
        in_specs=placed,
        out_specs=(P(("dp", "mp"), None), P("dp", "mp"), P("dp", "mp"), P("dp", "mp")),
        check_vma=False,
    )
```

```python
import jax
import jax.numpy as jnp
from jax import lax
from jax.experimental import pallas as pl
from jax.experimental.pallas import tpu as pltpu
from jax.sharding import PartitionSpec as P

MESH = pl.DeviceIdType.MESH
F32 = jnp.float32
BF16 = jnp.bfloat16
NZ, NY = 8, 4
EPS = 1e-06

SPAN = {"A0": (0, 1536), "A1": (1536, 2688), "H0": (2688, 4992), "H1": (4992, 6144)}
SUMS = {"A0": (0, 768), "A1": (768, 2688), "H0": (2688, 3840), "H1": (3840, 6144)}
A_COLS, H_COLS = 2688, 3456
STEPS = [("f", k) for k in (1, 2, 3, 4)] + [("b", k) for k in (1, 2, 3)]

NAMES = (
    [f"xo{g}" for g in SPAN]
    + [f"t{g}{w}{k}" for g in SPAN for w, k in STEPS]
    + [f"p{g}{w}{k}" for g in SUMS for w, k in STEPS]
    + [f"x{g}{w}{k}" for g in ("A0", "A1") for w, k in STEPS]
    + ["wx"]
    + [f"{n}{k}" for n in ("wf1", "wf2", "wb1", "ws0", "wsf1", "wsf2", "wsb1") for k in (0, 1)]
    + [f"px{g}{k}" for g in SUMS if g[0] == "A" for k in range(8)]
    + [f"fx{g}" for g in SUMS if g[0] == "H"]
    + [f"gs{k}" for k in range(8)]
    + [f"gy{k}" for k in range(6)]
    + ["gx"]
)
ID = {name: i for i, name in enumerate(NAMES)}

GATHER = (
    "A0f1", "A0b1", "A1f1", "oH0", "A1b1", "oH1", "A0f2", "A0b2",
    "A1f2", "wf10", "H0f1", "H0b1", "wb10", "A1b2", "H1f1", "H1b1",
    "wx", "A0f3", "A0b3", "wf20", "A1f3", "H0f2", "wf11", "H0b2",
    "A1b3", "H1f2", "H1b2", "A0f4", "A1f4", "wb11", "H0f3", "H0b3",
    "wf21", "H1f3", "H1b3", "H0f4", "H1f4",
)
SUM = (
    "PH0", "PA0", "G21", "PH1", "A0f0", "A0b0", "H0f1", "H0b1",
    "PA1", "D21", "G31", "H1f1", "G11", "G20", "G01", "G30",
    "H1b1", "A0f1", "G00", "A0b1", "A1f0", "G10", "D31", "H0f2",
    "A1b0", "H0b2", "D11", "H1f2", "D20", "H1b2", "A0f2", "A0b2",
    "A1f1", "H0f3", "A1b1", "D01", "D30", "H1f3", "A0f3", "A1f2",
    "D10", "H0pre", "A1b2", "H1pre", "A0fin", "H0fin", "A1f3", "D00",
    "A1fin", "H1fin",
)


def dot(a, b, contract):
    return lax.dot_general(a, b, (contract, ((), ())), preferred_element_type=F32)


def unit(rows):
    centred = rows - jnp.mean(rows, axis=-1, keepdims=True)
    inv = lax.rsqrt(jnp.mean(centred * centred, axis=-1, keepdims=True) + EPS)
    return centred * inv, inv


def unit_back(grad, rows_unit, inv, gain):
    e = grad * gain
    inner = jnp.mean(e * rows_unit, axis=-1, keepdims=True)
    return (e - jnp.mean(e, axis=-1, keepdims=True) - rows_unit * inner) * inv


def kernel(
    tok_in, gain, qg, kg, wq, wk, wv, gh,
    out_tok, out_q, out_k, out_v,
    tok, nrm, wts, part, gwt, rzh, rza, rxa, rxh, rs, ry, rh, acc, grd, grt, go, gsum, send, recv, local,
):
    d, m = lax.axis_index("dp"), lax.axis_index("mp")
    core, y, xh = lax.rem(d, 2), lax.rem(d // 2, NY), d // (2 * NY)
    z, xl = m // 2, lax.rem(m, 2)
    s = 1 - 2 * core

    def zo(o):
        return lax.rem(z + o * s + NZ, NZ)

    def yo(o):
        return lax.rem(y + o * s + NY, NY)

    def dp(x_other, yy, c=core):
        return ((lax.rem(xh + x_other, 2)) * NY + yy) * 2 + c

    to_zf, to_zb, to_x = (d, zo(1) * 2 + xl), (d, zo(-1) * 2 + xl), (d, z * 2 + 1 - xl)
    to_yf, to_yb = (dp(0, yo(1)), m), (dp(0, yo(-1)), m)
    to_s, to_h = (dp(0, y, 1 - core), m), (dp(1, y), m)
    started = []

    def put(name, src, dst, device, land=None):
        copy = pltpu.make_async_remote_copy(
            src_ref=src, dst_ref=dst, send_sem=send.at[ID[name]], recv_sem=recv.at[ID[land or name]],
            device_id=device, device_id_type=MESH,
        )
        copy.start()
        started.append(copy)

    def got(name, dst):
        pltpu.make_async_remote_copy(
            src_ref=dst, dst_ref=dst, send_sem=send.at[ID[name]], recv_sem=recv.at[ID[name]],
            device_id=to_s, device_id_type=MESH,
        ).wait_recv()

    tok_copy = pltpu.make_async_copy(tok_in, tok, local.at[4])
    tok_copy.start()
    own = [
        pltpu.make_async_copy(w, wts.at[d, :, pl.ds(256 * i, 256)], local.at[i])
        for i, w in enumerate((wq, wk, wv))
    ]
    for copy in own:
        copy.start()
    heads_in = pltpu.make_async_copy(gh, go, local.at[3])
    heads_in.start()

    barrier = pltpu.get_barrier_semaphore()
    for device in (to_zf, to_zb, to_x, to_yf, to_yb, to_s, to_h):
        pl.semaphore_signal(barrier, inc=1, device_id=device, device_id_type=MESH)

    tok_copy.wait()
    rows, _ = unit(tok[...].astype(F32))
    nrm[z, xl] = (rows * gain[...]).astype(BF16)
    pl.semaphore_wait(barrier, 7)

    def span(g):
        return pl.ds(SPAN[g][0], SPAN[g][1] - SPAN[g][0])

    def tokens_at(g, zz):
        return nrm.at[zz, xl, :, span(g)] if g[0] == "A" else nrm.at[zz, :, :, span(g)]

    def put_same(name, block, device):
        put(name, block, block, device)

    def put_w(name, block, device):
        put(name, wts.at[block], wts.at[block], device)

    def put_x(g):
        put_same(f"xo{g}", nrm.at[z, xl, :, span(g)], to_x)

    def put_z(g):
        put_same(f"t{g}f1", tokens_at(g, z), to_zf)
        put_same(f"t{g}b1", tokens_at(g, z), to_zb)

    def tokens_step(g, way, k):
        block = tokens_at(g, zo(-k if way == "f" else k))
        got(f"t{g}{way}{k}", block)
        if k < (4 if way == "f" else 3):
            put_same(f"t{g}{way}{k + 1}", block, to_zf if way == "f" else to_zb)
        if g[0] == "A":
            put_same(f"x{g}{way}{k}", block, to_x)

    def weights_step(kind, x):
        block = dp(x, yo({"f1": -1, "f2": -2, "b1": 1}[kind]))
        got(f"w{kind}{x}", wts.at[block])
        if kind == "f1":
            put_w(f"wf2{x}", block, to_yf)
        put_w(f"ws{kind}{x}", block, to_s)

    put_x("H0")
    put_z("A0")
    put_z("A1")
    for copy in own:
        copy.wait()
    put_w("wf10", d, to_yf)
    put_w("wb10", d, to_yb)
    put_x("H1")
    put_w("wx", d, to_h)
    put_w("ws00", d, to_s)
    put_x("A0")
    put_x("A1")
    for event in GATHER:
        if event[0] == "o":
            got(f"x{event}", nrm.at[z, 1 - xl, :, span(event[1:])])
            put_z(event[1:])
        elif event == "wx":
            block = dp(1, y)
            got("wx", wts.at[block])
            put_w("wf11", block, to_yf)
            put_w("wb11", block, to_yb)
            put_w("ws01", block, to_s)
        elif event[0] == "w":
            weights_step(event[1:3], int(event[3]))
        else:
            tokens_step(event[:2], event[2], int(event[3]))
    for g in ("A0", "A1"):
        got(f"xo{g}", nrm.at[z, 1 - xl, :, span(g)])
        for way, k in STEPS:
            got(f"x{g}{way}{k}", nrm.at[zo(-k if way == "f" else k), 1 - xl, :, span(g)])
    for x in (0, 1):
        got(f"ws0{x}", wts.at[dp(x, y, 1 - core)])
        got(f"wsf1{x}", wts.at[dp(x, yo(1), 1 - core)])
        got(f"wsb1{x}", wts.at[dp(x, yo(-1), 1 - core)])
        got(f"wsf2{x}", wts.at[dp(x, yo(2), 1 - core)])

    def columns(j):
        start = pl.multiple_of(j * 768, 768)
        return nrm[:, :, :, pl.ds(start, 768)].reshape(512, 768)

    @pl.loop(0, 2)
    def _(image):
        rows = nrm[pl.ds(4 * image, 4)].reshape(256, 6144)
        r = pl.ds(pl.multiple_of(256 * image, 256), 256)
        acc[r] = dot(rows, wts[...].reshape(6144, 768), ((1,), (0,)))

    heads_in.wait()
    q_gain, k_gain = qg[...], kg[...]

    for image in (0, 1):
        r = slice(image * 256, image * 256 + 256)
        for h in (0, 1):
            q_unit, q_inv = unit(acc[r, h * 128 : h * 128 + 128])
            k_unit, k_inv = unit(acc[r, 256 + h * 128 : 384 + h * 128])
            value = acc[r, 512 + h * 128 : 640 + h * 128].astype(BF16)
            qn, kn = (q_unit * q_gain).astype(BF16), (k_unit * k_gain).astype(BF16)
            cot = go[r, h * 128 : h * 128 + 128]
            scores = dot(qn, kn, ((1,), (1,))) * (128**-0.5)
            e = jnp.exp(scores - jnp.max(scores, axis=-1, keepdims=True))
            att = e / jnp.sum(e, axis=-1, keepdims=True)
            grad_v = dot(att.astype(BF16), cot, ((0,), (0,)))
            grad_p = dot(cot, value, ((1,), (1,)))
            delta = jnp.sum(att * grad_p, axis=-1, keepdims=True)
            grad_s = (att * (grad_p - delta) * (128**-0.5)).astype(BF16)
            grad_q = unit_back(dot(grad_s, kn, ((1,), (0,))), q_unit, q_inv, q_gain)
            grad_k = unit_back(dot(grad_s, qn, ((0,), (0,))), k_unit, k_inv, k_gain)
            for i, g in enumerate((grad_q, grad_k, grad_v)):
                c0 = i * 256 + h * 128
                grd[r, c0 : c0 + 128] = g.astype(BF16)
                grt[c0 : c0 + 128, r] = g.T.astype(BF16)

    def cols_of(g):
        return pl.ds(SUMS[g][0], SUMS[g][1] - SUMS[g][0])

    offsets = (4, -3, 3, -2, 2, -1, 1, 0)

    def make_part(g):
        first, last = SUMS[g][0] // 384, SUMS[g][1] // 384
        blocks = 2 if (last - first) % 2 == 0 else last - first
        width = blocks * 384

        @pl.loop(0, (last - first) // blocks)
        def _(i):
            w = wts[pl.ds(first + i * blocks, blocks)].reshape(width, 768)
            cols = pl.ds(pl.multiple_of(SUMS[g][0] + i * width, 128), width)
            part[:, :, :, cols] = dot(grd[...], w, ((1,), (1,))).astype(BF16).reshape(8, 2, 32, width)

        if g[0] == "A":
            for o in offsets:
                put(f"px{g}{o % 8}", part.at[zo(o), 1 - xl, :, cols_of(g)], rxa.at[o % 8, :, cols_of(g)], to_x)
        else:
            chain(g, "f", 0)
            chain(g, "b", 0)

    def make_gw(o, x):
        j = lax.rem(xh + x, 2) * NY + yo(o)
        p = dot(grt[...], columns(j), ((1,), (0,))).astype(BF16)
        gwt[2 * j] = p[:, :384]
        gwt[2 * j + 1] = p[:, 384:]
        there = (-o % 4) * 2 + x
        put(f"gs{(o % 4) * 2 + x}", gwt.at[2 * j + 1 - core], rs.at[there], to_s, f"gs{there}")

    def add(dst, *terms):
        total = dst[...].astype(F32)
        for t in terms:
            total = total + t[...].astype(F32)
        dst[...] = total.astype(BF16)

    def landing(g, way, k):
        slot = k - 1 if way == "f" else 3 + k
        start, end = SUMS[g]
        if g[0] == "A":
            return rza.at[slot, :, pl.ds(start, end - start)]
        return rzh.at[slot, :, :, pl.ds(start - A_COLS, end - start)]

    def chain(g, way, k):
        o = 4 - k if way == "f" else k - 3
        block = part.at[zo(o), xl, :, cols_of(g)] if g[0] == "A" else part.at[zo(o), :, :, cols_of(g)]
        terms = []
        if g[0] == "A":
            got(f"px{g}{o % 8}", rxa.at[o % 8, :, cols_of(g)])
            terms.append(rxa.at[o % 8, :, cols_of(g)])
        if k > 0:
            got(f"p{g}{way}{k}", landing(g, way, k))
            terms.append(landing(g, way, k))
        if terms:
            add(block, *terms)
        put(f"p{g}{way}{k + 1}", block, landing(g, way, k + 1), to_zf if way == "f" else to_zb)

    def chain_end(g):
        got(f"p{g}b3", landing(g, "b", 3))
        got(f"p{g}f4", landing(g, "f", 4))
        if g[0] == "H":
            block = part.at[z, 1 - xl, :, cols_of(g)]
            add(block, landing(g, "b", 3).at[1 - xl], landing(g, "f", 4).at[1 - xl])
            put(f"fx{g}", block, rxh.at[:, pl.ds(SUMS[g][0] - A_COLS, SUMS[g][1] - SUMS[g][0])], to_x)

    def finish_tokens(g):
        back, ahead = landing(g, "b", 3), landing(g, "f", 4)
        if g[0] == "A":
            chain_end(g)
            over = rxa.at[0, :, cols_of(g)]
            got(f"px{g}0", over)
        else:
            back, ahead = back.at[xl], ahead.at[xl]
            over = rxh.at[:, pl.ds(SUMS[g][0] - A_COLS, SUMS[g][1] - SUMS[g][0])]
            got(f"fx{g}", over)
        total = part[z, xl, :, cols_of(g)].astype(F32) + back[...].astype(F32)
        gsum[:, cols_of(g)] = total + ahead[...].astype(F32) + over[...].astype(F32)

    def add_gw(o, x):
        slot = (o % 4) * 2 + x
        got(f"gs{slot}", rs.at[slot])
        arrivals = {1: (x,), 0: (2 + x, 4 + x)}.get(o, ())
        for n in arrivals:
            got(f"gy{n}", ry.at[n])
        if o == 0 and x == 0:
            got("gx", rh)
            for i, out in enumerate((out_q, out_k, out_v)):
                r = pl.ds(256 * i, 256)
                total = gwt[d, r].astype(F32) + rs[0, r].astype(F32)
                total += ry[2, r].astype(F32) + ry[4, r].astype(F32) + rh[r].astype(F32)
                out[...] = total.T.astype(BF16)
            return
        block = gwt.at[dp(x, yo(o))]

        @pl.loop(0, 3)
        def _(i):
            r = pl.ds(pl.multiple_of(i * 256, 256), 256)
            add(block.at[r], rs.at[slot, r], *[ry.at[n, r] for n in arrivals])

        if o == 0:
            put("gx", block, rh, to_h)
        else:
            n = {2: 0, 1: 2, -1: 4}[o] + x
            put(f"gy{n}", block, ry.at[n], to_yb if o == -1 else to_yf)

    for event in SUM:
        if event[0] == "P":
            make_part(event[1:])
        elif event[0] in "GD":
            (make_gw if event[0] == "G" else add_gw)({"3": -1}.get(event[1], int(event[1])), int(event[2]))
        elif event[2:] == "pre":
            chain_end(event[:2])
        elif event[2:] == "fin":
            finish_tokens(event[:2])
        else:
            chain(event[:2], event[2], int(event[3]))

    rows, inv = unit(tok[...].astype(F32))
    out_tok[...] = unit_back(gsum[...], rows, inv, gain[...]).astype(BF16)

    for copy in started:
        copy.wait_send()


def hand_on(*refs):
    ins, outs, sems = refs[:4], refs[4:8], refs[8]
    copies = [pltpu.make_async_copy(a, b, sems.at[i]) for i, (a, b) in enumerate(zip(ins, outs))]
    for copy in copies:
        copy.start()
    for copy in copies:
        copy.wait()


def per_device(tokens, norm_gain, q_gain, k_gain, w_query, w_key, w_value, grad_heads):
    vmem, anywhere = pl.BlockSpec(memory_space=pltpu.VMEM), pl.BlockSpec(memory_space=pl.ANY)
    count = len(NAMES)
    shapes = [jax.ShapeDtypeStruct(a.shape, BF16) for a in (tokens, w_query, w_key, w_value)]
    results = pl.pallas_call(
        kernel,
        out_shape=shapes,
        in_specs=[anywhere] + [vmem] * 3 + [anywhere] * 4,
        out_specs=[vmem] * 4,
        scratch_shapes=[
            pltpu.VMEM((32, 6144), BF16),
            pltpu.VMEM((8, 2, 32, 6144), BF16),
            pltpu.VMEM((16, 384, 768), BF16),
            pltpu.VMEM((8, 2, 32, 6144), BF16),
            pltpu.VMEM((16, 768, 384), BF16),
            pltpu.VMEM((7, 2, 32, H_COLS), BF16),
            pltpu.VMEM((7, 32, A_COLS), BF16),
            pltpu.VMEM((8, 32, A_COLS), BF16),
            pltpu.VMEM((32, H_COLS), BF16),
            pltpu.VMEM((8, 768, 384), BF16),
            pltpu.VMEM((6, 768, 384), BF16),
            pltpu.VMEM((768, 384), BF16),
            pltpu.VMEM((512, 768), F32),
            pltpu.VMEM((512, 768), BF16),
            pltpu.VMEM((768, 512), BF16),
            pltpu.VMEM((512, 256), BF16),
            pltpu.VMEM((32, 6144), F32),
            pltpu.SemaphoreType.DMA((count,)),
            pltpu.SemaphoreType.DMA((count,)),
            pltpu.SemaphoreType.DMA((5,)),
        ],
        compiler_params=pltpu.CompilerParams(
            collective_id=0, has_side_effects=True, vmem_limit_bytes=64 * 1024 * 1024 - 65536
        ),
        cost_estimate=pl.CostEstimate(flops=15_000_000_000, bytes_accessed=3_000_000, transcendentals=300_000),
        name="attention_branch_back",
    )(
        tokens, norm_gain.reshape(1, -1), q_gain.reshape(1, -1), k_gain.reshape(1, -1),
        w_query, w_key, w_value, grad_heads,
    )
    return pl.pallas_call(
        hand_on,
        out_shape=shapes,
        in_specs=[vmem] * 4,
        out_specs=[anywhere] * 4,
        scratch_shapes=[pltpu.SemaphoreType.DMA((4,))],
        name="hand_on",
    )(*results)


def solution(mesh):
    placed = (
        P(("dp", "mp"), None),
        P(),
        P(),
        P(),
        P("dp", "mp"),
        P("dp", "mp"),
        P("dp", "mp"),
        P("dp", "mp"),
    )
    return jax.shard_map(
        per_device,
        mesh=mesh,
        in_specs=placed,
        out_specs=(P(("dp", "mp"), None), P("dp", "mp"), P("dp", "mp"), P("dp", "mp")),
        check_vma=False,
    )
```

```python
import jax
import jax.numpy as jnp
from jax import lax
from jax.experimental import pallas as pl
from jax.experimental.pallas import tpu as pltpu
from jax.sharding import PartitionSpec as P

MESH = pl.DeviceIdType.MESH
F32 = jnp.float32
BF16 = jnp.bfloat16
NZ, NY = 8, 4
EPS = 1e-06

SPAN = {"A0": (0, 1536), "A1": (1536, 2688), "H0": (2688, 4992), "H1": (4992, 6144)}
SUMS = {"A0": (0, 768), "A1": (768, 2688), "H0": (2688, 3840), "H1": (3840, 6144)}
A_COLS, H_COLS = 2688, 3456
STEPS = [("f", k) for k in (1, 2, 3, 4)] + [("b", k) for k in (1, 2, 3)]

NAMES = (
    [f"xo{g}" for g in SPAN]
    + [f"t{g}{w}{k}" for g in SPAN for w, k in STEPS]
    + [f"p{g}{w}{k}" for g in SUMS for w, k in STEPS]
    + [f"x{g}{w}{k}" for g in ("A0", "A1") for w, k in STEPS]
    + ["wx"]
    + [f"{n}{k}" for n in ("wf1", "wf2", "wb1", "ws0", "wsf1", "wsf2", "wsb1") for k in (0, 1)]
    + [f"px{g}{k}" for g in SUMS if g[0] == "A" for k in range(8)]
    + [f"fx{g}" for g in SUMS if g[0] == "H"]
    + [f"gs{k}" for k in range(8)]
    + [f"gy{k}" for k in range(6)]
    + ["gx"]
)
ID = {name: i for i, name in enumerate(NAMES)}

GATHER = (
    "A0f1", "A0b1", "A1f1", "oH0", "A1b1", "oH1", "A0f2", "A0b2",
    "A1f2", "wf10", "H0f1", "H0b1", "wb10", "A1b2", "H1f1", "H1b1",
    "wx", "A0f3", "A0b3", "wf20", "A1f3", "H0f2", "wf11", "H0b2",
    "A1b3", "H1f2", "H1b2", "A0f4", "A1f4", "wb11", "near1", "H0f3", "H0b3",
    "wf21", "H1f3", "H1b3", "near2", "H0f4", "H1f4",
)
SUM = (
    "PH0", "PA0", "G21", "PH1", "A0f0", "A0b0", "H0f1", "H0b1",
    "PA1", "D21", "G31", "G11", "G20", "H1f1", "G01", "G30",
    "H1b1", "A0f1", "A0b1", "A1f0", "D31", "G00", "G10", "H0f2",
    "A1b0", "H0b2", "D11", "D20", "H1f2", "D30", "H1b2", "A0f2",
    "A0b2", "A1f1", "H0f3", "A1b1", "D01", "H1f3", "A0f3", "A1f2",
    "A1b2", "H0pre", "D10", "H1pre", "A0fin", "H0fin", "A1f3", "A1fin",
    "D00", "H1fin",
)


def dot(a, b, contract):
    return lax.dot_general(a, b, (contract, ((), ())), preferred_element_type=F32)


def unit(rows):
    centred = rows - jnp.mean(rows, axis=-1, keepdims=True)
    inv = lax.rsqrt(jnp.mean(centred * centred, axis=-1, keepdims=True) + EPS)
    return centred * inv, inv


def unit_back(grad, rows_unit, inv, gain):
    e = grad * gain
    inner = jnp.mean(e * rows_unit, axis=-1, keepdims=True)
    return (e - jnp.mean(e, axis=-1, keepdims=True) - rows_unit * inner) * inv


def kernel(
    tok_in, gain, qg, kg, wq, wk, wv, gh,
    out_tok, out_q, out_k, out_v,
    tok, nrm, wts, part, gwt, rzh, rza, rxa, rxh, rs, ry, rh, acc, grd, grt, go, gsum, send, recv, local,
):
    d, m = lax.axis_index("dp"), lax.axis_index("mp")
    core, y, xh = lax.rem(d, 2), lax.rem(d // 2, NY), d // (2 * NY)
    z, xl = m // 2, lax.rem(m, 2)
    s = 1 - 2 * core

    def zo(o):
        return lax.rem(z + o * s + NZ, NZ)

    def yo(o):
        return lax.rem(y + o * s + NY, NY)

    def dp(x_other, yy, c=core):
        return ((lax.rem(xh + x_other, 2)) * NY + yy) * 2 + c

    to_zf, to_zb, to_x = (d, zo(1) * 2 + xl), (d, zo(-1) * 2 + xl), (d, z * 2 + 1 - xl)
    to_yf, to_yb = (dp(0, yo(1)), m), (dp(0, yo(-1)), m)
    to_s, to_h = (dp(0, y, 1 - core), m), (dp(1, y), m)
    started = []

    def put(name, src, dst, device, land=None):
        copy = pltpu.make_async_remote_copy(
            src_ref=src, dst_ref=dst, send_sem=send.at[ID[name]], recv_sem=recv.at[ID[land or name]],
            device_id=device, device_id_type=MESH,
        )
        copy.start()
        started.append(copy)

    def got(name, dst):
        pltpu.make_async_remote_copy(
            src_ref=dst, dst_ref=dst, send_sem=send.at[ID[name]], recv_sem=recv.at[ID[name]],
            device_id=to_s, device_id_type=MESH,
        ).wait_recv()

    tok_copy = pltpu.make_async_copy(tok_in, tok, local.at[4])
    tok_copy.start()
    own = [
        pltpu.make_async_copy(w, wts.at[d, :, pl.ds(256 * i, 256)], local.at[i])
        for i, w in enumerate((wq, wk, wv))
    ]
    for copy in own:
        copy.start()
    heads_in = pltpu.make_async_copy(gh, go, local.at[3])
    heads_in.start()

    barrier = pltpu.get_barrier_semaphore()
    for device in (to_zf, to_zb, to_x, to_yf, to_yb, to_s, to_h):
        pl.semaphore_signal(barrier, inc=1, device_id=device, device_id_type=MESH)

    tok_copy.wait()
    rows, _ = unit(tok[...].astype(F32))
    nrm[z, xl] = (rows * gain[...]).astype(BF16)
    pl.semaphore_wait(barrier, 7)

    def span(g):
        return pl.ds(SPAN[g][0], SPAN[g][1] - SPAN[g][0])

    def tokens_at(g, zz):
        return nrm.at[zz, xl, :, span(g)] if g[0] == "A" else nrm.at[zz, :, :, span(g)]

    def put_same(name, block, device):
        put(name, block, block, device)

    def put_w(name, block, device):
        put(name, wts.at[block], wts.at[block], device)

    def put_x(g):
        put_same(f"xo{g}", nrm.at[z, xl, :, span(g)], to_x)

    def put_z(g):
        put_same(f"t{g}f1", tokens_at(g, z), to_zf)
        put_same(f"t{g}b1", tokens_at(g, z), to_zb)

    def tokens_step(g, way, k):
        block = tokens_at(g, zo(-k if way == "f" else k))
        got(f"t{g}{way}{k}", block)
        if k < (4 if way == "f" else 3):
            put_same(f"t{g}{way}{k + 1}", block, to_zf if way == "f" else to_zb)
        if g[0] == "A":
            put_same(f"x{g}{way}{k}", block, to_x)

    def weights_step(kind, x):
        block = dp(x, yo({"f1": -1, "f2": -2, "b1": 1}[kind]))
        got(f"w{kind}{x}", wts.at[block])
        if kind == "f1":
            put_w(f"wf2{x}", block, to_yf)
        put_w(f"ws{kind}{x}", block, to_s)

    def columns(j):
        start = pl.multiple_of(j * 768, 768)
        return nrm[:, :, :, pl.ds(start, 768)].reshape(512, 768)

    def over_x(*ks):
        for g in ("A0", "A1"):
            for way, k in STEPS:
                if k in ks:
                    got(f"x{g}{way}{k}", nrm.at[zo(-k if way == "f" else k), 1 - xl, :, span(g)])

    def project_near(chips, first=False):
        for n, (x, o) in enumerate(chips):
            j = lax.rem(xh + x, 2) * NY + yo(o)
            cols = pl.ds(pl.multiple_of(j * 768, 768), 768)
            left = [nrm[zo(q), :, :, cols].reshape(64, 768) for q in (0, 1, 2, -2, -1)]
            p = dot(jnp.concatenate(left, axis=0), wts[pl.ds(2 * j, 2)].reshape(768, 768), ((1,), (0,)))
            if first and n == 0:
                acc[0:3] = p[:192].reshape(3, 64, 768)
                acc[6:8] = p[192:].reshape(2, 64, 768)
            else:
                acc[0:3] += p[:192].reshape(3, 64, 768)
                acc[6:8] += p[192:].reshape(2, 64, 768)

    def sibling_weights(kinds, x):
        for kind in kinds:
            got(f"ws{kind}{x}", wts.at[dp(x, yo({"0": 0, "f1": 1, "b1": -1, "f2": 2}[kind]), 1 - core)])

    put_x("H0")
    put_z("A0")
    put_z("A1")
    for copy in own:
        copy.wait()
    put_w("wf10", d, to_yf)
    put_w("wb10", d, to_yb)
    put_x("H1")
    put_w("wx", d, to_h)
    put_w("ws00", d, to_s)
    put_x("A0")
    put_x("A1")
    for event in GATHER:
        if event == "near1":
            for g in ("A0", "A1"):
                got(f"xo{g}", nrm.at[z, 1 - xl, :, span(g)])
            over_x(1, 2)
            sibling_weights(("0", "f1", "b1", "f2"), 0)
            sibling_weights(("0",), 1)
            project_near(((0, 0), (0, 1), (0, -1), (1, 0), (0, 2)), first=True)
        elif event == "near2":
            sibling_weights(("f1", "b1"), 1)
            project_near(((1, 1), (1, -1)))
        elif event[0] == "o":
            got(f"x{event}", nrm.at[z, 1 - xl, :, span(event[1:])])
            put_z(event[1:])
        elif event == "wx":
            block = dp(1, y)
            got("wx", wts.at[block])
            put_w("wf11", block, to_yf)
            put_w("wb11", block, to_yb)
            put_w("ws01", block, to_s)
        elif event[0] == "w":
            weights_step(event[1:3], int(event[3]))
        else:
            tokens_step(event[:2], event[2], int(event[3]))
    over_x(3, 4)
    got("wsf21", wts.at[dp(1, yo(2), 1 - core)])
    far = jnp.concatenate([nrm[zo(q)].reshape(64, 6144) for q in (3, 4, -3)], axis=0)
    acc[3:6] = dot(far, wts[...].reshape(6144, 768), ((1,), (0,))).reshape(3, 64, 768)
    project_near(((1, 2),))

    heads_in.wait()
    q_gain, k_gain = qg[...], kg[...]

    def projected(image, column):
        places = [lax.rem((4 * image + i - z) * s + NZ, NZ) for i in range(4)]
        return jnp.concatenate([acc[at, :, column : column + 128] for at in places], axis=0)


    for image in (0, 1):
        r = slice(image * 256, image * 256 + 256)
        for h in (0, 1):
            q_unit, q_inv = unit(projected(image, h * 128))
            k_unit, k_inv = unit(projected(image, 256 + h * 128))
            value = projected(image, 512 + h * 128).astype(BF16)
            qn, kn = (q_unit * q_gain).astype(BF16), (k_unit * k_gain).astype(BF16)
            cot = go[r, h * 128 : h * 128 + 128]
            scores = dot(qn, kn, ((1,), (1,))) * (128**-0.5)
            e = jnp.exp(scores - jnp.max(scores, axis=-1, keepdims=True))
            att = e / jnp.sum(e, axis=-1, keepdims=True)
            grad_v = dot(att.astype(BF16), cot, ((0,), (0,)))
            grad_p = dot(cot, value, ((1,), (1,)))
            delta = jnp.sum(att * grad_p, axis=-1, keepdims=True)
            grad_s = (att * (grad_p - delta) * (128**-0.5)).astype(BF16)
            grad_q = unit_back(dot(grad_s, kn, ((1,), (0,))), q_unit, q_inv, q_gain)
            grad_k = unit_back(dot(grad_s, qn, ((0,), (0,))), k_unit, k_inv, k_gain)
            for i, g in enumerate((grad_q, grad_k, grad_v)):
                c0 = i * 256 + h * 128
                grd[r, c0 : c0 + 128] = g.astype(BF16)
                grt[c0 : c0 + 128, r] = g.T.astype(BF16)

    def cols_of(g):
        return pl.ds(SUMS[g][0], SUMS[g][1] - SUMS[g][0])

    offsets = (4, -3, 3, -2, 2, -1, 1, 0)

    def make_part(g):
        first, last = SUMS[g][0] // 384, SUMS[g][1] // 384
        blocks = 2 if (last - first) % 2 == 0 else last - first
        width = blocks * 384

        @pl.loop(0, (last - first) // blocks)
        def _(i):
            w = wts[pl.ds(first + i * blocks, blocks)].reshape(width, 768)
            cols = pl.ds(pl.multiple_of(SUMS[g][0] + i * width, 128), width)
            part[:, :, :, cols] = dot(grd[...], w, ((1,), (1,))).astype(BF16).reshape(8, 2, 32, width)

        if g[0] == "A":
            for o in offsets:
                put(f"px{g}{o % 8}", part.at[zo(o), 1 - xl, :, cols_of(g)], rxa.at[o % 8, :, cols_of(g)], to_x)
        else:
            chain(g, "f", 0)
            chain(g, "b", 0)

    def make_gw(o, x):
        j = lax.rem(xh + x, 2) * NY + yo(o)
        p = dot(grt[...], columns(j), ((1,), (0,))).astype(BF16)
        gwt[2 * j] = p[:, :384]
        gwt[2 * j + 1] = p[:, 384:]
        there = (-o % 4) * 2 + x
        put(f"gs{(o % 4) * 2 + x}", gwt.at[2 * j + 1 - core], rs.at[there], to_s, f"gs{there}")

    def add(dst, *terms):
        total = dst[...].astype(F32)
        for t in terms:
            total = total + t[...].astype(F32)
        dst[...] = total.astype(BF16)

    def landing(g, way, k):
        slot = k - 1 if way == "f" else 3 + k
        start, end = SUMS[g]
        if g[0] == "A":
            return rza.at[slot, :, pl.ds(start, end - start)]
        return rzh.at[slot, :, :, pl.ds(start - A_COLS, end - start)]

    def chain(g, way, k):
        o = 4 - k if way == "f" else k - 3
        block = part.at[zo(o), xl, :, cols_of(g)] if g[0] == "A" else part.at[zo(o), :, :, cols_of(g)]
        terms = []
        if g[0] == "A":
            got(f"px{g}{o % 8}", rxa.at[o % 8, :, cols_of(g)])
            terms.append(rxa.at[o % 8, :, cols_of(g)])
        if k > 0:
            got(f"p{g}{way}{k}", landing(g, way, k))
            terms.append(landing(g, way, k))
        if terms:
            add(block, *terms)
        put(f"p{g}{way}{k + 1}", block, landing(g, way, k + 1), to_zf if way == "f" else to_zb)

    def chain_end(g):
        got(f"p{g}b3", landing(g, "b", 3))
        got(f"p{g}f4", landing(g, "f", 4))
        if g[0] == "H":
            block = part.at[z, 1 - xl, :, cols_of(g)]
            add(block, landing(g, "b", 3).at[1 - xl], landing(g, "f", 4).at[1 - xl])
            put(f"fx{g}", block, rxh.at[:, pl.ds(SUMS[g][0] - A_COLS, SUMS[g][1] - SUMS[g][0])], to_x)

    def finish_tokens(g):
        back, ahead = landing(g, "b", 3), landing(g, "f", 4)
        if g[0] == "A":
            chain_end(g)
            over = rxa.at[0, :, cols_of(g)]
            got(f"px{g}0", over)
        else:
            back, ahead = back.at[xl], ahead.at[xl]
            over = rxh.at[:, pl.ds(SUMS[g][0] - A_COLS, SUMS[g][1] - SUMS[g][0])]
            got(f"fx{g}", over)
        total = part[z, xl, :, cols_of(g)].astype(F32) + back[...].astype(F32)
        gsum[:, cols_of(g)] = total + ahead[...].astype(F32) + over[...].astype(F32)

    def add_gw(o, x):
        slot = (o % 4) * 2 + x
        got(f"gs{slot}", rs.at[slot])
        arrivals = {1: (x,), 0: (2 + x, 4 + x)}.get(o, ())
        for n in arrivals:
            got(f"gy{n}", ry.at[n])
        if o == 0 and x == 0:
            got("gx", rh)
            for i, out in enumerate((out_q, out_k, out_v)):
                r = pl.ds(256 * i, 256)
                total = gwt[d, r].astype(F32) + rs[0, r].astype(F32)
                total += ry[2, r].astype(F32) + ry[4, r].astype(F32) + rh[r].astype(F32)
                out[...] = total.T.astype(BF16)
            return
        block = gwt.at[dp(x, yo(o))]

        @pl.loop(0, 3)
        def _(i):
            r = pl.ds(pl.multiple_of(i * 256, 256), 256)
            add(block.at[r], rs.at[slot, r], *[ry.at[n, r] for n in arrivals])

        if o == 0:
            put("gx", block, rh, to_h)
        else:
            n = {2: 0, 1: 2, -1: 4}[o] + x
            put(f"gy{n}", block, ry.at[n], to_yb if o == -1 else to_yf)

    for event in SUM:
        if event[0] == "P":
            make_part(event[1:])
        elif event[0] in "GD":
            (make_gw if event[0] == "G" else add_gw)({"3": -1}.get(event[1], int(event[1])), int(event[2]))
        elif event[2:] == "pre":
            chain_end(event[:2])
        elif event[2:] == "fin":
            finish_tokens(event[:2])
        else:
            chain(event[:2], event[2], int(event[3]))

    rows, inv = unit(tok[...].astype(F32))
    out_tok[...] = unit_back(gsum[...], rows, inv, gain[...]).astype(BF16)

    for copy in started:
        copy.wait_send()


def hand_on(*refs):
    ins, outs, sems = refs[:4], refs[4:8], refs[8]
    copies = [pltpu.make_async_copy(a, b, sems.at[i]) for i, (a, b) in enumerate(zip(ins, outs))]
    for copy in copies:
        copy.start()
    for copy in copies:
        copy.wait()


def per_device(tokens, norm_gain, q_gain, k_gain, w_query, w_key, w_value, grad_heads):
    vmem, anywhere = pl.BlockSpec(memory_space=pltpu.VMEM), pl.BlockSpec(memory_space=pl.ANY)
    count = len(NAMES)
    shapes = [jax.ShapeDtypeStruct(a.shape, BF16) for a in (tokens, w_query, w_key, w_value)]
    results = pl.pallas_call(
        kernel,
        out_shape=shapes,
        in_specs=[anywhere] + [vmem] * 3 + [anywhere] * 4,
        out_specs=[vmem] * 4,
        scratch_shapes=[
            pltpu.VMEM((32, 6144), BF16),
            pltpu.VMEM((8, 2, 32, 6144), BF16),
            pltpu.VMEM((16, 384, 768), BF16),
            pltpu.VMEM((8, 2, 32, 6144), BF16),
            pltpu.VMEM((16, 768, 384), BF16),
            pltpu.VMEM((7, 2, 32, H_COLS), BF16),
            pltpu.VMEM((7, 32, A_COLS), BF16),
            pltpu.VMEM((8, 32, A_COLS), BF16),
            pltpu.VMEM((32, H_COLS), BF16),
            pltpu.VMEM((8, 768, 384), BF16),
            pltpu.VMEM((6, 768, 384), BF16),
            pltpu.VMEM((768, 384), BF16),
            pltpu.VMEM((8, 64, 768), F32),
            pltpu.VMEM((512, 768), BF16),
            pltpu.VMEM((768, 512), BF16),
            pltpu.VMEM((512, 256), BF16),
            pltpu.VMEM((32, 6144), F32),
            pltpu.SemaphoreType.DMA((count,)),
            pltpu.SemaphoreType.DMA((count,)),
            pltpu.SemaphoreType.DMA((5,)),
        ],
        compiler_params=pltpu.CompilerParams(
            collective_id=0, has_side_effects=True, vmem_limit_bytes=64 * 1024 * 1024 - 65536
        ),
        cost_estimate=pl.CostEstimate(flops=15_000_000_000, bytes_accessed=3_000_000, transcendentals=300_000),
        name="attention_branch_back",
    )(
        tokens, norm_gain.reshape(1, -1), q_gain.reshape(1, -1), k_gain.reshape(1, -1),
        w_query, w_key, w_value, grad_heads,
    )
    return pl.pallas_call(
        hand_on,
        out_shape=shapes,
        in_specs=[vmem] * 4,
        out_specs=[anywhere] * 4,
        scratch_shapes=[pltpu.SemaphoreType.DMA((4,))],
        name="hand_on",
    )(*results)


def solution(mesh):
    placed = (
        P(("dp", "mp"), None),
        P(),
        P(),
        P(),
        P("dp", "mp"),
        P("dp", "mp"),
        P("dp", "mp"),
        P("dp", "mp"),
    )
    return jax.shard_map(
        per_device,
        mesh=mesh,
        in_specs=placed,
        out_specs=(P(("dp", "mp"), None), P("dp", "mp"), P("dp", "mp"), P("dp", "mp")),
        check_vma=False,
    )
```

```python
import jax
import jax.numpy as jnp
from jax import lax
from jax.experimental import pallas as pl
from jax.experimental.pallas import tpu as pltpu
from jax.sharding import PartitionSpec as P

MESH = pl.DeviceIdType.MESH
F32 = jnp.float32
BF16 = jnp.bfloat16
NZ, NY = 8, 4
EPS = 1e-06

SPAN = {"A0": (0, 1536), "A1": (1536, 2688), "H0": (2688, 4992), "H1": (4992, 6144)}
SUMS = {"A0": (0, 768), "A1": (768, 2688), "H0": (2688, 3840), "H1": (3840, 6144)}
A_COLS, H_COLS = 2688, 3456
STEPS = [("f", k) for k in (1, 2, 3, 4)] + [("b", k) for k in (1, 2, 3)]

NAMES = (
    [f"xo{g}" for g in SPAN]
    + [f"t{g}{w}{k}" for g in SPAN for w, k in STEPS]
    + [f"p{g}{w}{k}" for g in SUMS for w, k in STEPS]
    + [f"x{g}{w}{k}" for g in ("A0", "A1") for w, k in STEPS]
    + ["wx"]
    + [f"{n}{k}" for n in ("wf1", "wf2", "wb1", "ws0", "wsf1", "wsf2", "wsb1") for k in (0, 1)]
    + [f"px{g}{k}" for g in SUMS if g[0] == "A" for k in range(8)]
    + [f"fx{g}" for g in SUMS if g[0] == "H"]
    + [f"gs{k}" for k in range(8)]
    + [f"gy{k}" for k in range(6)]
    + ["gx"]
)
ID = {name: i for i, name in enumerate(NAMES)}

GATHER = (
    "A0f1", "A0b1", "A1f1", "oH0", "A1b1", "oH1", "A0f2", "A0b2",
    "A1f2", "wf10", "H0f1", "H0b1", "wb10", "A1b2", "H1f1", "H1b1",
    "wx", "A0f3", "A0b3", "wf20", "A1f3", "H0f2", "wf11", "H0b2",
    "A1b3", "H1f2", "H1b2", "A0f4", "A1f4", "wb11", "near1", "H0f3", "H0b3",
    "wf21", "H1f3", "H1b3", "near2", "H0f4", "H1f4",
)
SUM = (
    "PH0", "PA0", "G21", "PH1", "A0f0", "A0b0", "H0f1", "H0b1",
    "PA1", "D21", "G31", "G11", "G20", "H1f1", "G01", "G30",
    "H1b1", "A0f1", "A0b1", "A1f0", "D31", "G00", "G10", "H0f2",
    "A1b0", "H0b2", "D11", "D20", "H1f2", "D30", "H1b2", "A0f2",
    "A0b2", "A1f1", "H0f3", "A1b1", "D01", "H1f3", "A0f3", "A1f2",
    "A1b2", "H0pre", "D10", "H1pre", "A0fin", "H0fin", "A1f3", "A1fin",
    "D00", "H1fin",
)


def dot(a, b, contract):
    return lax.dot_general(a, b, (contract, ((), ())), preferred_element_type=F32)


def unit(rows):
    centred = rows - jnp.mean(rows, axis=-1, keepdims=True)
    inv = lax.rsqrt(jnp.mean(centred * centred, axis=-1, keepdims=True) + EPS)
    return centred * inv, inv


def unit_back(grad, rows_unit, inv, gain):
    e = grad * gain
    inner = jnp.mean(e * rows_unit, axis=-1, keepdims=True)
    return (e - jnp.mean(e, axis=-1, keepdims=True) - rows_unit * inner) * inv


def kernel(
    tok_in, gain, qg, kg, wq, wk, wv, gh,
    out_tok, out_q, out_k, out_v,
    tok, nrm, wts, part, gwt, rzh, rza, rxa, rxh, rs, ry, rh, acc, grd, grt, go, gsum, send, recv, local,
):
    d, m = lax.axis_index("dp"), lax.axis_index("mp")
    core, y, xh = lax.rem(d, 2), lax.rem(d // 2, NY), d // (2 * NY)
    z, xl = m // 2, lax.rem(m, 2)
    s = 1 - 2 * core

    def zo(o):
        return lax.rem(z + o * s + NZ, NZ)

    def yo(o):
        return lax.rem(y + o * s + NY, NY)

    def dp(x_other, yy, c=core):
        return ((lax.rem(xh + x_other, 2)) * NY + yy) * 2 + c

    to_zf, to_zb, to_x = (d, zo(1) * 2 + xl), (d, zo(-1) * 2 + xl), (d, z * 2 + 1 - xl)
    to_yf, to_yb = (dp(0, yo(1)), m), (dp(0, yo(-1)), m)
    to_s, to_h = (dp(0, y, 1 - core), m), (dp(1, y), m)
    started = []

    def put(name, src, dst, device, land=None):
        copy = pltpu.make_async_remote_copy(
            src_ref=src, dst_ref=dst, send_sem=send.at[ID[name]], recv_sem=recv.at[ID[land or name]],
            device_id=device, device_id_type=MESH,
        )
        copy.start()
        started.append(copy)

    def got(name, dst):
        pltpu.make_async_remote_copy(
            src_ref=dst, dst_ref=dst, send_sem=send.at[ID[name]], recv_sem=recv.at[ID[name]],
            device_id=to_s, device_id_type=MESH,
        ).wait_recv()

    tok_copy = pltpu.make_async_copy(tok_in, tok, local.at[4])
    tok_copy.start()
    own = [
        pltpu.make_async_copy(w, wts.at[d, :, pl.ds(256 * i, 256)], local.at[i])
        for i, w in enumerate((wq, wk, wv))
    ]
    for copy in own:
        copy.start()
    heads_in = pltpu.make_async_copy(gh, go, local.at[3])
    heads_in.start()

    barrier = pltpu.get_barrier_semaphore()
    for device in (to_zf, to_zb, to_x, to_yf, to_yb, to_s, to_h):
        pl.semaphore_signal(barrier, inc=1, device_id=device, device_id_type=MESH)

    tok_copy.wait()
    rows, _ = unit(tok[...].astype(F32))
    nrm[z, xl] = (rows * gain[...]).astype(BF16)
    pl.semaphore_wait(barrier, 7)

    def span(g):
        return pl.ds(SPAN[g][0], SPAN[g][1] - SPAN[g][0])

    def tokens_at(g, zz):
        return nrm.at[zz, xl, :, span(g)] if g[0] == "A" else nrm.at[zz, :, :, span(g)]

    def put_same(name, block, device):
        put(name, block, block, device)

    def put_w(name, block, device):
        put(name, wts.at[block], wts.at[block], device)

    def put_x(g):
        put_same(f"xo{g}", nrm.at[z, xl, :, span(g)], to_x)

    def put_z(g):
        put_same(f"t{g}f1", tokens_at(g, z), to_zf)
        put_same(f"t{g}b1", tokens_at(g, z), to_zb)

    def tokens_step(g, way, k):
        block = tokens_at(g, zo(-k if way == "f" else k))
        got(f"t{g}{way}{k}", block)
        if k < (4 if way == "f" else 3):
            put_same(f"t{g}{way}{k + 1}", block, to_zf if way == "f" else to_zb)
        if g[0] == "A":
            put_same(f"x{g}{way}{k}", block, to_x)

    def weights_step(kind, x):
        block = dp(x, yo({"f1": -1, "f2": -2, "b1": 1}[kind]))
        got(f"w{kind}{x}", wts.at[block])
        if kind == "f1":
            put_w(f"wf2{x}", block, to_yf)
        put_w(f"ws{kind}{x}", block, to_s)

    def columns(j):
        start = pl.multiple_of(j * 768, 768)
        return nrm[:, :, :, pl.ds(start, 768)].reshape(512, 768)

    def over_x(*ks):
        for g in ("A0", "A1"):
            for way, k in STEPS:
                if k in ks:
                    got(f"x{g}{way}{k}", nrm.at[zo(-k if way == "f" else k), 1 - xl, :, span(g)])

    def project_near(chips, first=False):
        for n, (x, o) in enumerate(chips):
            j = lax.rem(xh + x, 2) * NY + yo(o)
            cols = pl.ds(pl.multiple_of(j * 768, 768), 768)
            left = [nrm[zo(q), :, :, cols].reshape(64, 768) for q in (0, 1, 2, -2, -1)]
            p = dot(jnp.concatenate(left, axis=0), wts[pl.ds(2 * j, 2)].reshape(768, 768), ((1,), (0,)))
            if first and n == 0:
                acc[0:3] = p[:192].reshape(3, 64, 768)
                acc[6:8] = p[192:].reshape(2, 64, 768)
            else:
                acc[0:3] += p[:192].reshape(3, 64, 768)
                acc[6:8] += p[192:].reshape(2, 64, 768)

    def sibling_weights(kinds, x):
        for kind in kinds:
            got(f"ws{kind}{x}", wts.at[dp(x, yo({"0": 0, "f1": 1, "b1": -1, "f2": 2}[kind]), 1 - core)])

    put_x("H0")
    put_z("A0")
    put_z("A1")
    for copy in own:
        copy.wait()
    put_w("wf10", d, to_yf)
    put_w("wb10", d, to_yb)
    put_x("H1")
    put_w("wx", d, to_h)
    put_w("ws00", d, to_s)
    put_x("A0")
    put_x("A1")
    for event in GATHER:
        if event == "near1":
            for g in ("A0", "A1"):
                got(f"xo{g}", nrm.at[z, 1 - xl, :, span(g)])
            over_x(1, 2)
            sibling_weights(("0", "f1", "b1", "f2"), 0)
            sibling_weights(("0",), 1)
            project_near(((0, 0), (0, 1), (0, -1), (1, 0), (0, 2)), first=True)
        elif event == "near2":
            sibling_weights(("f1", "b1"), 1)
            project_near(((1, 1), (1, -1)))
            sibling_weights(("f2",), 1)
            project_near(((1, 2),))
        elif event[0] == "o":
            got(f"x{event}", nrm.at[z, 1 - xl, :, span(event[1:])])
            put_z(event[1:])
        elif event == "wx":
            block = dp(1, y)
            got("wx", wts.at[block])
            put_w("wf11", block, to_yf)
            put_w("wb11", block, to_yb)
            put_w("ws01", block, to_s)
        elif event[0] == "w":
            weights_step(event[1:3], int(event[3]))
        else:
            tokens_step(event[:2], event[2], int(event[3]))
    over_x(3, 4)
    far = jnp.concatenate([nrm[zo(q)].reshape(64, 6144) for q in (3, 4, -3)], axis=0)
    acc[3:6] = dot(far, wts[...].reshape(6144, 768), ((1,), (0,))).reshape(3, 64, 768)

    heads_in.wait()
    q_gain, k_gain = qg[...], kg[...]

    def projected(image, column):
        places = [lax.rem((4 * image + i - z) * s + NZ, NZ) for i in range(4)]
        return jnp.concatenate([acc[at, :, column : column + 128] for at in places], axis=0)


    for image in (0, 1):
        r = slice(image * 256, image * 256 + 256)
        for h in (0, 1):
            q_unit, q_inv = unit(projected(image, h * 128))
            k_unit, k_inv = unit(projected(image, 256 + h * 128))
            value = projected(image, 512 + h * 128).astype(BF16)
            qn, kn = (q_unit * q_gain).astype(BF16), (k_unit * k_gain).astype(BF16)
            cot = go[r, h * 128 : h * 128 + 128]
            scores = dot(qn, kn, ((1,), (1,))) * (128**-0.5)
            e = jnp.exp(scores - jnp.max(scores, axis=-1, keepdims=True))
            att = e / jnp.sum(e, axis=-1, keepdims=True)
            grad_v = dot(att.astype(BF16), cot, ((0,), (0,)))
            grad_p = dot(cot, value, ((1,), (1,)))
            delta = jnp.sum(att * grad_p, axis=-1, keepdims=True)
            grad_s = (att * (grad_p - delta) * (128**-0.5)).astype(BF16)
            grad_q = unit_back(dot(grad_s, kn, ((1,), (0,))), q_unit, q_inv, q_gain)
            grad_k = unit_back(dot(grad_s, qn, ((0,), (0,))), k_unit, k_inv, k_gain)
            for i, g in enumerate((grad_q, grad_k, grad_v)):
                c0 = i * 256 + h * 128
                grd[r, c0 : c0 + 128] = g.astype(BF16)
                grt[c0 : c0 + 128, r] = g.T.astype(BF16)

    def cols_of(g):
        return pl.ds(SUMS[g][0], SUMS[g][1] - SUMS[g][0])

    offsets = (4, -3, 3, -2, 2, -1, 1, 0)

    def make_part(g):
        first, last = SUMS[g][0] // 384, SUMS[g][1] // 384
        blocks = 2 if (last - first) % 2 == 0 else last - first
        width = blocks * 384

        @pl.loop(0, (last - first) // blocks)
        def _(i):
            w = wts[pl.ds(first + i * blocks, blocks)].reshape(width, 768)
            cols = pl.ds(pl.multiple_of(SUMS[g][0] + i * width, 128), width)
            part[:, :, :, cols] = dot(grd[...], w, ((1,), (1,))).astype(BF16).reshape(8, 2, 32, width)

        if g[0] == "A":
            for o in offsets:
                put(f"px{g}{o % 8}", part.at[zo(o), 1 - xl, :, cols_of(g)], rxa.at[o % 8, :, cols_of(g)], to_x)
        else:
            chain(g, "f", 0)
            chain(g, "b", 0)

    def make_gw(o, x):
        j = lax.rem(xh + x, 2) * NY + yo(o)
        p = dot(grt[...], columns(j), ((1,), (0,))).astype(BF16)
        gwt[2 * j] = p[:, :384]
        gwt[2 * j + 1] = p[:, 384:]
        there = (-o % 4) * 2 + x
        put(f"gs{(o % 4) * 2 + x}", gwt.at[2 * j + 1 - core], rs.at[there], to_s, f"gs{there}")

    def add(dst, *terms):
        total = dst[...].astype(F32)
        for t in terms:
            total = total + t[...].astype(F32)
        dst[...] = total.astype(BF16)

    def landing(g, way, k):
        slot = k - 1 if way == "f" else 3 + k
        start, end = SUMS[g]
        if g[0] == "A":
            return rza.at[slot, :, pl.ds(start, end - start)]
        return rzh.at[slot, :, :, pl.ds(start - A_COLS, end - start)]

    def chain(g, way, k):
        o = 4 - k if way == "f" else k - 3
        block = part.at[zo(o), xl, :, cols_of(g)] if g[0] == "A" else part.at[zo(o), :, :, cols_of(g)]
        terms = []
        if g[0] == "A":
            got(f"px{g}{o % 8}", rxa.at[o % 8, :, cols_of(g)])
            terms.append(rxa.at[o % 8, :, cols_of(g)])
        if k > 0:
            got(f"p{g}{way}{k}", landing(g, way, k))
            terms.append(landing(g, way, k))
        if terms:
            add(block, *terms)
        put(f"p{g}{way}{k + 1}", block, landing(g, way, k + 1), to_zf if way == "f" else to_zb)

    def chain_end(g):
        got(f"p{g}b3", landing(g, "b", 3))
        got(f"p{g}f4", landing(g, "f", 4))
        if g[0] == "H":
            block = part.at[z, 1 - xl, :, cols_of(g)]
            add(block, landing(g, "b", 3).at[1 - xl], landing(g, "f", 4).at[1 - xl])
            put(f"fx{g}", block, rxh.at[:, pl.ds(SUMS[g][0] - A_COLS, SUMS[g][1] - SUMS[g][0])], to_x)

    def finish_tokens(g):
        back, ahead = landing(g, "b", 3), landing(g, "f", 4)
        if g[0] == "A":
            chain_end(g)
            over = rxa.at[0, :, cols_of(g)]
            got(f"px{g}0", over)
        else:
            back, ahead = back.at[xl], ahead.at[xl]
            over = rxh.at[:, pl.ds(SUMS[g][0] - A_COLS, SUMS[g][1] - SUMS[g][0])]
            got(f"fx{g}", over)
        total = part[z, xl, :, cols_of(g)].astype(F32) + back[...].astype(F32)
        gsum[:, cols_of(g)] = total + ahead[...].astype(F32) + over[...].astype(F32)

    def add_gw(o, x):
        slot = (o % 4) * 2 + x
        got(f"gs{slot}", rs.at[slot])
        arrivals = {1: (x,), 0: (2 + x, 4 + x)}.get(o, ())
        for n in arrivals:
            got(f"gy{n}", ry.at[n])
        if o == 0 and x == 0:
            got("gx", rh)
            for i, out in enumerate((out_q, out_k, out_v)):
                r = pl.ds(256 * i, 256)
                total = gwt[d, r].astype(F32) + rs[0, r].astype(F32)
                total += ry[2, r].astype(F32) + ry[4, r].astype(F32) + rh[r].astype(F32)
                out[...] = total.T.astype(BF16)
            return
        block = gwt.at[dp(x, yo(o))]

        @pl.loop(0, 3)
        def _(i):
            r = pl.ds(pl.multiple_of(i * 256, 256), 256)
            add(block.at[r], rs.at[slot, r], *[ry.at[n, r] for n in arrivals])

        if o == 0:
            put("gx", block, rh, to_h)
        else:
            n = {2: 0, 1: 2, -1: 4}[o] + x
            put(f"gy{n}", block, ry.at[n], to_yb if o == -1 else to_yf)

    for event in SUM:
        if event[0] == "P":
            make_part(event[1:])
        elif event[0] in "GD":
            (make_gw if event[0] == "G" else add_gw)({"3": -1}.get(event[1], int(event[1])), int(event[2]))
        elif event[2:] == "pre":
            chain_end(event[:2])
        elif event[2:] == "fin":
            finish_tokens(event[:2])
        else:
            chain(event[:2], event[2], int(event[3]))

    rows, inv = unit(tok[...].astype(F32))
    out_tok[...] = unit_back(gsum[...], rows, inv, gain[...]).astype(BF16)

    for copy in started:
        copy.wait_send()


def hand_on(*refs):
    ins, outs, sems = refs[:4], refs[4:8], refs[8]
    copies = [pltpu.make_async_copy(a, b, sems.at[i]) for i, (a, b) in enumerate(zip(ins, outs))]
    for copy in copies:
        copy.start()
    for copy in copies:
        copy.wait()


def per_device(tokens, norm_gain, q_gain, k_gain, w_query, w_key, w_value, grad_heads):
    vmem, anywhere = pl.BlockSpec(memory_space=pltpu.VMEM), pl.BlockSpec(memory_space=pl.ANY)
    count = len(NAMES)
    shapes = [jax.ShapeDtypeStruct(a.shape, BF16) for a in (tokens, w_query, w_key, w_value)]
    results = pl.pallas_call(
        kernel,
        out_shape=shapes,
        in_specs=[anywhere] + [vmem] * 3 + [anywhere] * 4,
        out_specs=[vmem] * 4,
        scratch_shapes=[
            pltpu.VMEM((32, 6144), BF16),
            pltpu.VMEM((8, 2, 32, 6144), BF16),
            pltpu.VMEM((16, 384, 768), BF16),
            pltpu.VMEM((8, 2, 32, 6144), BF16),
            pltpu.VMEM((16, 768, 384), BF16),
            pltpu.VMEM((7, 2, 32, H_COLS), BF16),
            pltpu.VMEM((7, 32, A_COLS), BF16),
            pltpu.VMEM((8, 32, A_COLS), BF16),
            pltpu.VMEM((32, H_COLS), BF16),
            pltpu.VMEM((8, 768, 384), BF16),
            pltpu.VMEM((6, 768, 384), BF16),
            pltpu.VMEM((768, 384), BF16),
            pltpu.VMEM((8, 64, 768), F32),
            pltpu.VMEM((512, 768), BF16),
            pltpu.VMEM((768, 512), BF16),
            pltpu.VMEM((512, 256), BF16),
            pltpu.VMEM((32, 6144), F32),
            pltpu.SemaphoreType.DMA((count,)),
            pltpu.SemaphoreType.DMA((count,)),
            pltpu.SemaphoreType.DMA((5,)),
        ],
        compiler_params=pltpu.CompilerParams(
            collective_id=0, has_side_effects=True, vmem_limit_bytes=64 * 1024 * 1024 - 65536
        ),
        cost_estimate=pl.CostEstimate(flops=15_000_000_000, bytes_accessed=3_000_000, transcendentals=300_000),
        name="attention_branch_back",
    )(
        tokens, norm_gain.reshape(1, -1), q_gain.reshape(1, -1), k_gain.reshape(1, -1),
        w_query, w_key, w_value, grad_heads,
    )
    return pl.pallas_call(
        hand_on,
        out_shape=shapes,
        in_specs=[vmem] * 4,
        out_specs=[anywhere] * 4,
        scratch_shapes=[pltpu.SemaphoreType.DMA((4,))],
        name="hand_on",
    )(*results)


def solution(mesh):
    placed = (
        P(("dp", "mp"), None),
        P(),
        P(),
        P(),
        P("dp", "mp"),
        P("dp", "mp"),
        P("dp", "mp"),
        P("dp", "mp"),
    )
    return jax.shard_map(
        per_device,
        mesh=mesh,
        in_specs=placed,
        out_specs=(P(("dp", "mp"), None), P("dp", "mp"), P("dp", "mp"), P("dp", "mp")),
        check_vma=False,
    )
```
